128 devices in a mesh: ctx: 32 (over y, z, core), head: 4 (over x).
Axes of the slice: x: 4, y: 4, z: 4, core: 2. Of those that a mesh axis runs over, the one named last changes fastest.
Arguments:
- queries: bfloat16 [65536, 2048], P('ctx', 'head'), may hold values from -8 to 6
- key_input: bfloat16 [65536, 2048], P('ctx', 'head'), may hold values from -8 to 6
- value_input: bfloat16 [65536, 2048], P('ctx', 'head'), may hold values from -6 to 6
- out_weight: bfloat16 [2048, 2048], P('head'), may hold values from -0.125 to 0.125
- cotangent: bfloat16 [65536, 2048], P('ctx', 'head'), may hold values from -6 to 6
Outputs:
- layer_out: bfloat16 [65536, 2048], P('ctx', 'head')
- grad_query: bfloat16 [65536, 2048], P('ctx', 'head')
- grad_key: bfloat16 [65536, 2048], P('ctx', 'head')
- grad_value: bfloat16 [65536, 2048], P('ctx', 'head')
The draws below stay inside these ranges and needn't reach their ends.
All inputs are finite; a program needn't handle non-finite values.
Results may differ from the reference program's by a relative error of at most 0.009.
Values may be sent and summed in bfloat16 or wider, within the bound.
No kernel may reach another device: no remote copies, remote signals or barrier semaphores. Data moves between devices by JAX's collectives and lax.ppermute only.
A program may use at most 192 MiB of HBM per device.

```python
import jax
import jax.numpy as jnp
from jax import lax

D = 2048
HEADS = 16
DH = 128
BLOCK = 512
TOKENS = 65536


def mix_features(active, on_values, off_values):
    return jnp.where(active, on_values, off_values).astype(jnp.bfloat16)


def draw_queries(key, part):
    key = jax.random.fold_in(key, 11)
    pick_key, on_key, off_key = jax.random.split(key, 3)
    shape = (TOKENS, HEADS * DH)
    active = jax.random.bernoulli(pick_key, 0.125, shape)
    on_values = jnp.clip(3.0 + jax.random.normal(on_key, shape, jnp.float32), 1.0, 5.0)
    off_values = jnp.clip(-5.0 + jax.random.normal(off_key, shape, jnp.float32), -7.0, -3.0)
    return mix_features(active, on_values, off_values)


def draw_key_input(key, part):
    key = jax.random.fold_in(key, 23)
    pick_key, on_key, off_key = jax.random.split(key, 3)
    shape = (TOKENS, HEADS * DH)
    active = jax.random.bernoulli(pick_key, 0.125, shape)
    on_values = jnp.clip(3.0 + jax.random.normal(on_key, shape, jnp.float32), 1.0, 5.0)
    off_values = jnp.clip(-5.0 + jax.random.normal(off_key, shape, jnp.float32), -7.0, -3.0)
    return mix_features(active, on_values, off_values)


def block_levels(key, shape, shards, least, largest):
    gain, own = 1.0, jax.random.fold_in(key, 6)
    for dim, shards_of in shards:
        steps = jnp.exp(jax.random.uniform(jax.random.fold_in(own, dim), (shards_of,), jnp.float32, least / len(shards), largest / len(shards)))
        gain = gain * jnp.repeat(steps, shape[dim] // shards_of).reshape([-1 if axis == dim else 1 for axis in range(len(shape))])
    return gain


def gaussian(own_key, dims, scale, most, pieces=(), held_as=jnp.bfloat16):
    values = jax.random.normal(own_key, dims, jnp.float32) * scale
    if len(pieces) > 0:
        values = block_levels(own_key, dims, pieces, -0.22, 0.18) * values
    return jnp.clip(values, min=-most, max=most).astype(held_as)


def setup_inputs(seed: int = 0) -> dict:
    key_list = jax.random.split(jax.random.key(seed), 6)
    queries = draw_queries(jax.random.fold_in(key_list[5], 71), 0)
    key_input = draw_key_input(jax.random.fold_in(key_list[5], 71), 0)
    value_input = gaussian(key_list[2], (TOKENS, HEADS * DH), 1.0, 6.0, ((0, 32), (1, 4)))
    out_weight = gaussian(key_list[3], (HEADS * DH, D), (HEADS * DH) ** -0.5, 0.125, ((0, 4),))
    cotangent = gaussian(key_list[4], (TOKENS, D), 1.0, 6.0, ((0, 32), (1, 4)))
    return {"queries": queries, "key_input": key_input, "value_input": value_input, "out_weight": out_weight, "cotangent": cotangent}


HIGH = lax.Precision.HIGHEST


def feature(inputs):
    lifted = inputs.astype(jnp.float32)
    return jnp.where(lifted > 0, lifted + 1.0, jnp.exp(jnp.minimum(lifted, 0.0)))


def slope(inputs):
    lifted = inputs.astype(jnp.float32)
    return jnp.where(lifted > 0, 1.0, jnp.exp(jnp.minimum(lifted, 0.0)))


def reference(queries, key_input, value_input, out_weight, cotangent):
    token_count, width = queries.shape
    head_count = width // DH
    blocks = token_count // BLOCK
    shape4 = (blocks, BLOCK, head_count, DH)
    feat_q = feature(queries).astype(jnp.bfloat16).reshape(shape4)
    feat_k = feature(key_input).astype(jnp.bfloat16).reshape(shape4)
    value_blocks = value_input.reshape(shape4)
    lower = lax.broadcasted_iota(jnp.int32, (BLOCK, BLOCK), 0) >= lax.broadcasted_iota(jnp.int32, (BLOCK, BLOCK), 1)

    def forward_step(carry, inputs):
        state_kv, state_z = carry
        query_block, key_block, value_block = inputs
        query_wide = query_block.astype(jnp.float32)
        key_wide = key_block.astype(jnp.float32)
        value_wide = value_block.astype(jnp.float32)
        scores = jnp.einsum('thd,shd->hts', query_wide, key_wide, precision=HIGH)
        masked = jnp.where(lower, scores, 0.0)
        weights = masked.astype(jnp.bfloat16)
        numer = jnp.einsum('hts,shd->thd', weights.astype(jnp.float32), value_wide, precision=HIGH)
        numer = numer + jnp.einsum('thd,hde->the', query_wide, state_kv, precision=HIGH)
        denom = jnp.sum(masked, -1).T + jnp.einsum('thd,hd->th', query_wide, state_z, precision=HIGH)
        attend = numer / denom[..., None]
        next_kv = state_kv + jnp.einsum('shd,she->hde', key_wide, value_wide, precision=HIGH)
        next_z = state_z + jnp.sum(key_wide, 0)
        return (next_kv, next_z), (attend, denom, state_kv, state_z)

    start = (jnp.zeros((head_count, DH, DH), jnp.float32), jnp.zeros((head_count, DH), jnp.float32))
    _, (attend, denom, kv_states, z_states) = lax.scan(forward_step, start, (feat_q, feat_k, value_blocks))
    attn_rows = attend.astype(jnp.bfloat16).reshape(token_count, width)
    layer_out = jnp.dot(attn_rows, out_weight, preferred_element_type=jnp.float32).astype(jnp.bfloat16)
    grad_attn = jnp.dot(cotangent, out_weight.T, preferred_element_type=jnp.float32).reshape(shape4)
    grad_num = (grad_attn / denom[..., None]).astype(jnp.bfloat16)
    grad_den = -jnp.sum(grad_attn * attend, -1) / denom

    def backward_step(carry, inputs):
        back_kv, back_z = carry
        query_block, key_block, value_block, num_block, den_block, state_kv, state_z = inputs
        query_wide = query_block.astype(jnp.float32)
        key_wide = key_block.astype(jnp.float32)
        value_wide = value_block.astype(jnp.float32)
        num_wide = num_block.astype(jnp.float32)
        scores = jnp.einsum('thd,shd->hts', query_wide, key_wide, precision=HIGH)
        weights = jnp.where(lower, scores, 0.0).astype(jnp.bfloat16).astype(jnp.float32)
        grad_score = jnp.einsum('the,she->hts', num_wide, value_wide, precision=HIGH) + den_block.T[:, :, None]
        grad_weight = jnp.where(lower, grad_score, 0.0).astype(jnp.bfloat16).astype(jnp.float32)
        grad_q = jnp.einsum('hts,shd->thd', grad_weight, key_wide, precision=HIGH)
        grad_q = grad_q + jnp.einsum('hde,the->thd', state_kv, num_wide, precision=HIGH) + den_block[..., None] * state_z[None]
        grad_k = jnp.einsum('hts,thd->shd', grad_weight, query_wide, precision=HIGH)
        grad_k = grad_k + jnp.einsum('hde,she->shd', back_kv, value_wide, precision=HIGH) + back_z[None]
        grad_v = jnp.einsum('hts,the->she', weights, num_wide, precision=HIGH)
        grad_v = grad_v + jnp.einsum('hde,shd->she', back_kv, key_wide, precision=HIGH)
        next_kv = back_kv + jnp.einsum('thd,the->hde', query_wide, num_wide, precision=HIGH)
        next_z = back_z + jnp.einsum('thd,th->hd', query_wide, den_block, precision=HIGH)
        return (next_kv, next_z), (grad_q, grad_k, grad_v)

    _, (grad_q, grad_k, grad_v) = lax.scan(backward_step, start, (feat_q, feat_k, value_blocks, grad_num, grad_den, kv_states, z_states), reverse=True)
    grad_query = (grad_q.reshape(token_count, width) * slope(queries)).astype(jnp.bfloat16)
    grad_key = (grad_k.reshape(token_count, width) * slope(key_input)).astype(jnp.bfloat16)
    grad_value = grad_v.reshape(token_count, width).astype(jnp.bfloat16)
    return (layer_out, grad_query, grad_key, grad_value)
```

```python
import functools

import jax
import jax.numpy as jnp
from jax import lax
from jax.experimental import pallas as pl
from jax.experimental.pallas import tpu as pltpu
from jax.sharding import PartitionSpec as P

DH = 128
BLOCK = 512
HALF = BLOCK // 2
NH = 4
NB = 4
ROWS = DH + 8
BF = jnp.bfloat16
F32 = jnp.float32

PARAMS = pltpu.CompilerParams(vmem_limit_bytes=56 * 1024 * 1024)

NN = (((1,), (0,)), ((), ()))
NT = (((1,), (1,)), ((), ()))
TN = (((0,), (0,)), ((), ()))


def dot(a, b, dims):
    return lax.dot_general(a, b, dims, preferred_element_type=F32)


def feature(lifted):
    return jnp.where(lifted > 0, lifted + 1.0, jnp.exp(jnp.minimum(lifted, 0.0)))


def slope(lifted):
    return jnp.where(lifted > 0, 1.0, jnp.exp(jnp.minimum(lifted, 0.0)))


def halves(state):
    upper = state.astype(BF)
    return upper, (state - upper.astype(F32)).astype(BF)


def cols(head):
    return slice(head * DH, (head + 1) * DH)


def totals_kernel(k_ref, v_ref, loc_ref, tot_ref):
    @pl.when(pl.program_id(0) == 0)
    def _():
        tot_ref[...] = jnp.zeros_like(tot_ref)

    for head in range(NH):
        feat = feature(k_ref[:, cols(head)].astype(F32)).astype(BF)
        kv = dot(v_ref[:, cols(head)], feat, TN)
        z = jnp.sum(feat.astype(F32), axis=0, keepdims=True)
        before = tot_ref[head]
        loc_ref[0, head] = before
        tot_ref[head, :DH] = before[:DH] + kv
        tot_ref[head, DH:] = before[DH:] + jnp.broadcast_to(z, (ROWS - DH, DH))


def totals(k, v):
    block = pl.BlockSpec((BLOCK, NH * DH), lambda b: (b, 0))
    return pl.pallas_call(
        totals_kernel,
        grid=(NB,),
        in_specs=[block, block],
        out_specs=[
            pl.BlockSpec((1, NH, ROWS, DH), lambda b: (b, 0, 0, 0)),
            pl.BlockSpec((NH, ROWS, DH), lambda b: (0, 0, 0)),
        ],
        out_shape=[
            jax.ShapeDtypeStruct((NB, NH, ROWS, DH), F32),
            jax.ShapeDtypeStruct((NH, ROWS, DH), F32),
        ],
        compiler_params=PARAMS,
        name="totals",
    )(k, v)


def causal():
    return lax.broadcasted_iota(jnp.int32, (HALF, HALF), 0) >= lax.broadcasted_iota(
        jnp.int32, (HALF, HALF), 1
    )


def attend_kernel(q0, q1, k0, k1, v0, v1, loc_ref, prior_ref, a0, a1, r0, r1):
    lower = causal()
    ones = jnp.ones((BLOCK, DH), BF)
    for block, (q_ref, k_ref, v_ref, a_ref, r_ref) in enumerate(
        ((q0, k0, v0, a0, r0), (q1, k1, v1, a1, r1))
    ):
        fq = feature(q_ref[...].astype(F32)).astype(BF)
        fk = feature(k_ref[...].astype(F32)).astype(BF)
        wide = jnp.concatenate([v_ref[...], ones], axis=1)
        state = prior_ref[0] + loc_ref[block, 0]
        both = jnp.concatenate(
            [state[:DH], jnp.broadcast_to(state[DH : DH + 1], (DH, DH))], axis=0
        )
        sums = jnp.concatenate(halves(both), axis=1)
        past = dot(jnp.concatenate([fq, fq], axis=1), sums, NT)
        w00 = jnp.where(lower, dot(fq[:HALF], fk[:HALF], NT), 0.0).astype(BF)
        w10 = dot(fq[HALF:], fk[:HALF], NT).astype(BF)
        w11 = jnp.where(lower, dot(fq[HALF:], fk[HALF:], NT), 0.0).astype(BF)
        top = past[:HALF] + dot(w00, wide[:HALF], NN)
        low = past[HALF:] + dot(jnp.concatenate([w10, w11], axis=1), wide, NN)
        for rows, res in ((slice(0, HALF), top), (slice(HALF, BLOCK), low)):
            inv = 1.0 / res[:, DH:]
            r_ref[rows] = inv
            a_ref[rows] = (res[:, :DH] * inv).astype(BF)


def attend_chunk(q, k, v, loc, prior, chunk):
    first = pl.BlockSpec((BLOCK, DH), lambda h: (2 * chunk, h))
    second = pl.BlockSpec((BLOCK, DH), lambda h: (2 * chunk + 1, h))
    own = pl.BlockSpec((BLOCK, DH), lambda h: (0, h))
    return pl.pallas_call(
        attend_kernel,
        grid=(NH,),
        in_specs=[first, second] * 3
        + [
            pl.BlockSpec((2, 1, ROWS, DH), lambda h: (chunk, h, 0, 0)),
            pl.BlockSpec((1, ROWS, DH), lambda h: (h, 0, 0)),
        ],
        out_specs=[own] * 4,
        out_shape=[jax.ShapeDtypeStruct((BLOCK, NH * DH), BF)] * 2
        + [jax.ShapeDtypeStruct((BLOCK, NH * DH), F32)] * 2,
        compiler_params=PARAMS,
        name="attend",
    )(q, q, k, k, v, v, loc, prior)


def project_kernel(
    dims, place, xa, xb, ga, gb, wh, wx, wd, am, ao, bm, bo, keep_a, keep_b, to_x, to_d
):
    even = place[3] == 0
    a_h = jnp.where(even, am[...], ao[...])
    a_d = jnp.where(even, ao[...], am[...])
    b_h = jnp.where(even, bm[...], bo[...])
    b_x = jnp.where(even, bo[...], bm[...])
    own = wh[...]
    if dims == NT:
        ka, sa, kb, sb = wx[...], (b_h, b_x), wd[...], (a_h, a_d)
    else:
        ka, sa, kb, sb = a_h, (wd[...], a_d), b_h, (wx[...], b_x)
    keep_a[...] = dot(xa[...], own, dims) + dot(ga[...], ka, dims)
    to_d[...] = (dot(xa[...], sa[0], dims) + dot(ga[...], sa[1], dims)).astype(BF)
    keep_b[...] = dot(xb[...], own, dims) + dot(gb[...], kb, dims)
    to_x[...] = (dot(xb[...], sb[0], dims) + dot(gb[...], sb[1], dims)).astype(BF)


def project(dims, place, xa, xb, offset, ga, gb, weight, remote, steps=2):
    size = NH * DH
    rows = BLOCK // steps
    tile = pl.BlockSpec((rows, size), lambda i, s: (i, 0))
    whole = pl.BlockSpec((size, size), lambda i, s: (0, 0))

    def part(slot):
        return pl.BlockSpec((size, size), lambda i, s: (0, s[slot]))

    def at(block):
        return pl.BlockSpec((rows, size), lambda i, s: (block * steps + i, 0))

    return pl.pallas_call(
        functools.partial(project_kernel, dims),
        grid_spec=pltpu.PrefetchScalarGridSpec(
            num_scalar_prefetch=1,
            grid=(steps,),
            in_specs=[at(offset[0]), at(offset[1]), tile, tile, part(0), part(1), part(2)]
            + [whole] * 4,
            out_specs=[tile] * 4,
        ),
        out_shape=[jax.ShapeDtypeStruct((BLOCK, size), F32)] * 2
        + [jax.ShapeDtypeStruct((BLOCK, size), BF)] * 2,
        compiler_params=PARAMS,
        name="project",
    )(place, xa, xb, ga, gb, weight, weight, weight, *remote)


def numden_kernel(q0, q1, a0, a1, r0, r1, k0, k1, p0, p1, gn_ref, den_ref, sum_ref):
    head = pl.program_id(0)
    lane = lax.broadcasted_iota(jnp.int32, (BLOCK, DH), 1)

    @pl.when(head == 0)
    def _():
        den_ref[...] = jnp.zeros_like(den_ref)

    for block, (q_ref, a_ref, r_ref, k_ref, p_ref) in enumerate(
        ((q0, a0, r0, k0, p0), (q1, a1, r1, k1, p1))
    ):
        rows = slice(block * BLOCK, (block + 1) * BLOCK)
        fq = feature(q_ref[...].astype(F32)).astype(BF)
        grad = k_ref[...] + p_ref[...].astype(F32)
        inv = r_ref[...]
        num = (grad * inv).astype(BF)
        gn_ref[rows] = num
        den = -jnp.sum(grad * a_ref[...].astype(F32), axis=1, keepdims=True) * inv
        upper = den.astype(BF)
        rest = (den - upper.astype(F32)).astype(BF)
        den_ref[rows] = jnp.where(
            lane == 2 * head, upper, jnp.where(lane == 2 * head + 1, rest, den_ref[rows])
        )
        sum_ref[block, 0, :DH] = dot(num, fq, TN)
        z = jnp.sum(den * fq.astype(F32), axis=0, keepdims=True)
        sum_ref[block, 0, DH:] = jnp.broadcast_to(z, (ROWS - DH, DH))


def numden(q, a, r, keep, got, chunk):
    first = pl.BlockSpec((BLOCK, DH), lambda h: (2 * chunk, h))
    second = pl.BlockSpec((BLOCK, DH), lambda h: (2 * chunk + 1, h))
    own = pl.BlockSpec((BLOCK, DH), lambda h: (0, h))
    return pl.pallas_call(
        numden_kernel,
        grid=(NH,),
        in_specs=[first, second] + [own] * 8,
        out_specs=[
            pl.BlockSpec((2 * BLOCK, DH), lambda h: (0, h)),
            pl.BlockSpec((2 * BLOCK, DH), lambda h: (0, 0)),
            pl.BlockSpec((2, 1, ROWS, DH), lambda h: (0, h, 0, 0)),
        ],
        out_shape=[
            jax.ShapeDtypeStruct((2 * BLOCK, NH * DH), BF),
            jax.ShapeDtypeStruct((2 * BLOCK, DH), BF),
            jax.ShapeDtypeStruct((2, NH, ROWS, DH), F32),
        ],
        compiler_params=PARAMS,
        name="numden",
    )(q, q, *a, *r, *keep, *got)


def local_kernel(q_ref, k_ref, v_ref, n_ref, d_ref, loc_ref, prior_ref, *rest):
    gq_ref, gk_ref, gv_ref = rest[-3:]
    upper = lax.broadcasted_iota(jnp.int32, (HALF, HALF), 0) <= lax.broadcasted_iota(
        jnp.int32, (HALF, HALF), 1
    )
    lane = lax.broadcasted_iota(jnp.int32, (BLOCK, DH), 1)
    top, low = slice(0, HALF), slice(HALF, BLOCK)
    dens = d_ref[...]
    for head in range(NH):
        col = cols(head)
        queries = q_ref[:, col].astype(F32)
        raw = feature(queries)
        fq = raw.astype(BF)
        fk = feature(k_ref[:, col].astype(F32)).astype(BF)
        num = n_ref[:, col]
        pick = ((lane == 2 * head) | (lane == 2 * head + 1)).astype(F32).astype(BF)
        left = jnp.concatenate([v_ref[:, col], pick], axis=1)
        right = jnp.concatenate([num, dens], axis=1)

        def pair(a, b, s, t, mask):
            out = dot(a[s], b[t], NT)
            return (jnp.where(upper, out, 0.0) if mask else out).astype(BF)

        w00 = pair(fk, fq, top, top, True)
        w01 = pair(fk, fq, top, low, False)
        w11 = pair(fk, fq, low, low, True)
        g00 = pair(left, right, top, top, True)
        g01 = pair(left, right, top, low, False)
        g11 = pair(left, right, low, low, True)
        gv_ref[top, col] = dot(jnp.concatenate([w00, w01], axis=1), num, NN)
        gv_ref[low, col] = dot(w11, num[low], NN)
        gk_ref[top, col] = dot(jnp.concatenate([g00, g01], axis=1), fq, NN)
        gk_ref[low, col] = dot(g11, fq[low], NN)
        state = prior_ref[head] + loc_ref[0, head]
        past = dot(
            jnp.concatenate([num, num], axis=1),
            jnp.concatenate(halves(state[:DH]), axis=0),
            NN,
        )
        den = dens[:, 2 * head : 2 * head + 1].astype(F32) + dens[
            :, 2 * head + 1 : 2 * head + 2
        ].astype(F32)
        past = past + den * state[DH : DH + 1]
        tilt = jnp.minimum(raw, 1.0)
        gq_ref[top, col] = (tilt[top] * (past[top] + dot(g00, fk[top], TN))).astype(BF)
        gq_ref[low, col] = (
            tilt[low]
            * (past[low] + dot(jnp.concatenate([g01, g11], axis=0), fk, TN))
        ).astype(BF)


def local(q, k, v, num, den, loc, prior, chunk, earlier):
    wide = pl.BlockSpec((BLOCK, NH * DH), lambda b: (2 * chunk + b, 0))
    near = pl.BlockSpec((BLOCK, NH * DH), lambda b: (b, 0))
    full = (NB * BLOCK, NH * DH)
    extra = () if earlier is None else tuple(earlier)
    return pl.pallas_call(
        local_kernel,
        grid=(2,),
        in_specs=[
            wide,
            wide,
            wide,
            near,
            pl.BlockSpec((BLOCK, DH), lambda b: (b, 0)),
            pl.BlockSpec((1, NH, ROWS, DH), lambda b: (2 * chunk + b, 0, 0, 0)),
            pl.BlockSpec((NH, ROWS, DH), lambda b: (0, 0, 0)),
        ]
        + [pl.BlockSpec(memory_space=pl.ANY)] * len(extra),
        out_specs=[wide] * 3,
        out_shape=[
            jax.ShapeDtypeStruct(full, BF),
            jax.ShapeDtypeStruct(full, F32),
            jax.ShapeDtypeStruct(full, F32),
        ],
        input_output_aliases={7 + i: i for i in range(len(extra))},
        compiler_params=PARAMS,
        name="local",
    )(q, k, v, num, den, loc, prior, *extra)


def later_kernel(k_ref, v_ref, gk_in, gv_in, s0_ref, s1_ref, after_ref, gk_ref, gv_ref):
    state = after_ref[0]
    for block in reversed(range(NB)):
        rows = slice(block * BLOCK, (block + 1) * BLOCK)
        raw = feature(k_ref[rows].astype(F32))
        fk = raw.astype(BF)
        upper, rest = halves(state[:DH])
        val = v_ref[rows]
        gk = gk_in[rows] + dot(
            jnp.concatenate([val, val], axis=1), jnp.concatenate([upper, rest], axis=0), NN
        )
        gk = gk + state[DH : DH + 1]
        gk_ref[rows] = (jnp.minimum(raw, 1.0) * gk).astype(BF)
        gv = gv_in[rows] + dot(
            jnp.concatenate([fk, fk], axis=1), jnp.concatenate([upper, rest], axis=1), NT
        )
        gv_ref[rows] = gv.astype(BF)
        if block:
            state = state + (s0_ref, s1_ref)[block // 2][block % 2, 0]


def later(k, v, gk, gv, s0, s1, after):
    tall = pl.BlockSpec((NB * BLOCK, DH), lambda h: (0, h))
    sums = pl.BlockSpec((2, 1, ROWS, DH), lambda h: (0, h, 0, 0))
    return pl.pallas_call(
        later_kernel,
        grid=(NH,),
        in_specs=[tall] * 4 + [sums, sums, pl.BlockSpec((1, ROWS, DH), lambda h: (h, 0, 0))],
        out_specs=[tall] * 2,
        out_shape=[jax.ShapeDtypeStruct((NB * BLOCK, NH * DH), BF)] * 2,
        compiler_params=PARAMS,
        name="later",
    )(k, v, gk, gv, s0, s1, after)


A_PAIRS = [(h, h ^ 1) for h in range(4)]
B_PAIRS = [(h, 3 - h) for h in range(4)]


def ctx_pairs(change):
    out = []
    for y in range(4):
        for z in range(4):
            for c in range(2):
                y2, z2, c2 = change(y, z, c)
                out.append((y * 8 + z * 2 + c, y2 * 8 + z2 * 2 + c2))
    return out


def swap(x, change):
    return lax.ppermute(x, "ctx", ctx_pairs(change))


def sibling(x):
    return swap(x, lambda y, z, c: (y, z, 1 - c))


def entering(total, reverse):
    index = lax.axis_index("ctx")
    core, z, y = index % 2, (index // 2) % 4, index // 8
    second_core = (core == 0) if reverse else (core == 1)
    odd_z = (z % 2 == 0) if reverse else (z % 2 == 1)
    high_z = (z < 2) if reverse else (z >= 2)
    odd_y = (y % 2 == 0) if reverse else (y % 2 == 1)
    high_y = (y < 2) if reverse else (y >= 2)
    parts = total.reshape(2, 2, ROWS, DH)
    mine = lax.dynamic_index_in_dim(parts, core, 0, False)
    other = lax.dynamic_index_in_dim(parts, 1 - core, 0, False)
    got = sibling(other)
    chip = mine + got
    near = swap(chip, lambda y, z, c: (y ^ 1, z, c))
    pair = chip + near
    far = swap(pair, lambda y, z, c: (3 - y, z, c))
    column = jnp.where(odd_y, near, 0.0) + jnp.where(high_y, far, 0.0)
    both = swap(jnp.stack([column, chip]), lambda y, z, c: (y, z ^ 1, c))
    column2 = column + both[0]
    chip2 = chip + both[1]
    message = column2 + jnp.where(high_z, 0.0, chip2)
    more = swap(message, lambda y, z, c: (y, 3 - z, c))
    ahead = column2 + jnp.where(odd_z, both[1], 0.0) + more
    my = ahead + jnp.where(second_core, got, 0.0)
    its = ahead + jnp.where(second_core, 0.0, mine)
    back = sibling(its)
    lower = jnp.where(core == 0, my, back)
    upper = jnp.where(core == 0, back, my)
    return jnp.concatenate([lower, upper], axis=0)


def on_device(queries, key_input, value_input, out_weight, cotangent):
    head = lax.axis_index("head")
    core = lax.axis_index("ctx") % 2
    size = NH * DH
    place = jnp.stack([head, head ^ 1, 3 - head, core]).astype(jnp.int32)

    def to_x(x):
        return lax.ppermute(x, "head", A_PAIRS)

    def to_d(x):
        return lax.ppermute(x, "head", B_PAIRS)

    def rows(x, block):
        return lax.slice_in_dim(x, block * BLOCK, (block + 1) * BLOCK, axis=0)

    partner, across = head ^ 1, 3 - head
    a_cols = jnp.where(core == 0, partner, 3 - partner) * size
    b_cols = jnp.where(core == 0, across, across ^ 1) * size
    a_mine = to_x(lax.dynamic_slice_in_dim(out_weight, a_cols, size, 1))
    b_mine = to_d(lax.dynamic_slice_in_dim(out_weight, b_cols, size, 1))
    remote = (a_mine, sibling(a_mine), b_mine, sibling(b_mine))

    cots = [(to_x(rows(cotangent, 2 * c)), to_d(rows(cotangent, 2 * c + 1))) for c in range(2)]
    loc, total = totals(key_input, value_input)
    prior = entering(total, False)

    grads = []
    for c in range(2):
        keep_a, keep_b, send_x, send_d = project(
            NT, place, cotangent, cotangent, (2 * c, 2 * c + 1), *cots[c], out_weight, remote
        )
        grads.append(((keep_a, keep_b), (to_d(send_d), to_x(send_x))))

    heads = [attend_chunk(queries, key_input, value_input, loc, prior, c) for c in range(2)]
    gathered = [(to_x(heads[c][0]), to_d(heads[c][1])) for c in range(2)]

    nums = [numden(queries, heads[c][:2], heads[c][2:], *grads[c], c) for c in range(2)]
    sums0, sums1 = nums[0][2], nums[1][2]
    after = entering(jnp.sum(sums0, 0) + jnp.sum(sums1, 0), True)

    outs = []
    for c in range(2):
        keep_a, keep_b, send_x, send_d = project(
            NN, place, heads[c][0], heads[c][1], (0, 0), *gathered[c], out_weight, remote
        )
        outs.append((keep_a + to_d(send_d).astype(F32)).astype(BF))
        outs.append((keep_b + to_x(send_x).astype(F32)).astype(BF))
    layer_out = jnp.concatenate(outs, axis=0)

    state = None
    for c in range(2):
        state = local(
            queries, key_input, value_input, nums[c][0], nums[c][1], loc, prior, c, state
        )
    grad_query, near_k, near_v = state
    grad_key, grad_value = later(
        key_input, value_input, near_k, near_v, sums0, sums1, after
    )
    return (layer_out, grad_query, grad_key, grad_value)


def solution(mesh):
    in_specs = (
        P("ctx", "head"),
        P("ctx", "head"),
        P("ctx", "head"),
        P("head", None),
        P("ctx", "head"),
    )
    out_specs = (P("ctx", "head"), P("ctx", "head"), P("ctx", "head"), P("ctx", "head"))
    return jax.shard_map(
        on_device, mesh=mesh, in_specs=in_specs, out_specs=out_specs, check_vma=False
    )
```

```python
import functools

import jax
import jax.numpy as jnp
from jax import lax
from jax.experimental import pallas as pl
from jax.experimental.pallas import tpu as pltpu
from jax.sharding import PartitionSpec as P

DH = 128
BLOCK = 512
HALF = BLOCK // 2
NH = 4
NB = 4
ROWS = DH + 8
BF = jnp.bfloat16
F32 = jnp.float32

PARAMS = pltpu.CompilerParams(vmem_limit_bytes=12 * 1024 * 1024)
VMEM = pl.BlockSpec(memory_space=pltpu.VMEM)
ANY = pl.BlockSpec(memory_space=pl.ANY)

NN = (((1,), (0,)), ((), ()))
NT = (((1,), (1,)), ((), ()))
TN = (((0,), (0,)), ((), ()))


def dot(a, b, dims):
    return lax.dot_general(a, b, dims, preferred_element_type=F32)


def feature(lifted):
    return jnp.where(lifted > 0, lifted + 1.0, jnp.exp(jnp.minimum(lifted, 0.0)))


def slope(lifted):
    return jnp.where(lifted > 0, 1.0, jnp.exp(jnp.minimum(lifted, 0.0)))


def halves(state):
    upper = state.astype(BF)
    return upper, (state - upper.astype(F32)).astype(BF)


def call(kernel, name, args, outs, after=(), aliases=None):
    count, extra = len(args), len(after)

    def body(*refs):
        kernel(*refs[:count], *refs[count + extra :])

    return pl.pallas_call(
        body,
        in_specs=[VMEM] * (count + extra),
        out_specs=[VMEM] * len(outs),
        out_shape=[pltpu.VMEM(shape, dtype) for shape, dtype in outs],
        input_output_aliases=aliases or {},
        compiler_params=PARAMS,
        name=name,
    )(*args, *after)


def place():
    head, index = lax.axis_index("head"), lax.axis_index("ctx")
    return head, index % 2, (index // 2) % 4, index // 8


def partner(head):
    return head + 1 - 2 * (head % 2)


def tie(x, *after):
    return lax.optimization_barrier((x, *after))[0] if after else x


def cols(head):
    return slice(head * DH, (head + 1) * DH)


def rows_of(block):
    return slice(block * BLOCK, (block + 1) * BLOCK)


def with_row(state, row):
    return jnp.concatenate([state, jnp.broadcast_to(row, (ROWS - DH, DH))], axis=0)


def stage(kernel, name, args, outs, after=()):
    count, extra = len(args), len(after)

    def body(*refs):
        sems = refs[-1]
        copies = [
            pltpu.make_async_copy(source, target, sems.at[i])
            for i, (source, target) in enumerate(
                zip(kernel(*refs[:count]), refs[count + extra : -1])
            )
        ]
        for copy in copies:
            copy.start()
        for copy in copies:
            copy.wait()

    return pl.pallas_call(
        body,
        in_specs=[ANY] * count + [VMEM] * extra,
        out_specs=[VMEM] * len(outs),
        out_shape=[pltpu.VMEM(shape, dtype) for shape, dtype in outs],
        scratch_shapes=[pltpu.SemaphoreType.DMA((len(outs),))],
        compiler_params=PARAMS,
        name=name,
    )(*args, *after)


def quarter(w_ref, index):
    size = NH * DH
    return w_ref.at[:, pl.ds(pl.multiple_of(index * size, size), size)]


def first_pieces(w_ref, c_ref):
    head, core, _, _ = place()
    x, d = partner(head), 3 - head
    return (
        quarter(w_ref, x + core * (3 - 2 * x)),
        quarter(w_ref, d + core * (partner(d) - d)),
        c_ref.at[rows_of(0)],
        c_ref.at[rows_of(1)],
    )


def second_pieces(w_ref, c_ref):
    head, _, _, _ = place()
    return (
        c_ref.at[rows_of(2)],
        c_ref.at[rows_of(3)],
        quarter(w_ref, head),
        quarter(w_ref, partner(head)),
        quarter(w_ref, 3 - head),
    )


HALF_STATE = (NH // 2, ROWS, DH)


def split(core, sums, mine_ref, other_ref):
    for i in range(NH // 2):
        low, high = sums[i], sums[NH // 2 + i]
        mine_ref[i] = jnp.where(core == 0, low, high)
        other_ref[i] = jnp.where(core == 0, high, low)


def whole(core, pair, head):
    mine, back = pair
    slot = head % (NH // 2)
    return jnp.where(core == head // (NH // 2), mine[slot], back[slot])


def totals_kernel(k_ref, v_ref, loc_ref, fk_ref, mine_ref, other_ref):
    _, core, _, _ = place()
    sums = []
    for head in range(NH):
        col = cols(head)
        total = jnp.zeros((ROWS, DH), F32)
        for block in range(NB):
            row = rows_of(block)
            feat = feature(k_ref[row, col].astype(F32)).astype(BF)
            fk_ref[row, col] = feat
            loc_ref[block, head] = total
            total = total + with_row(
                dot(v_ref[row, col], feat, TN),
                jnp.sum(feat.astype(F32), axis=0, keepdims=True),
            )
        sums.append(total)
    split(core, sums, mine_ref, other_ref)


def totals(k, v, after):
    return call(
        totals_kernel,
        "totals",
        (k, v),
        [((NB, NH, ROWS, DH), F32), ((NB * BLOCK, NH * DH), BF), (HALF_STATE, F32), (HALF_STATE, F32)],
        after,
    )


def inside_kernel(chunk, q_ref, k_ref, v_ref, f_ref, n_ref, d_ref):
    lower = lax.broadcasted_iota(jnp.int32, (HALF, HALF), 0) >= lax.broadcasted_iota(
        jnp.int32, (HALF, HALF), 1
    )
    ones = jnp.ones((BLOCK, DH), BF)
    for block in range(2):
        row = rows_of(2 * chunk + block)
        base = block * BLOCK
        for head in range(NH):
            col = cols(head)
            fq = feature(q_ref[row, col].astype(F32)).astype(BF)
            f_ref[base : base + BLOCK, col] = fq
            fk = k_ref[row, col]
            wide = jnp.concatenate([v_ref[row, col], ones], axis=1)
            w00 = jnp.where(lower, dot(fq[:HALF], fk[:HALF], NT), 0.0).astype(BF)
            w10 = dot(fq[HALF:], fk[:HALF], NT).astype(BF)
            w11 = jnp.where(lower, dot(fq[HALF:], fk[HALF:], NT), 0.0).astype(BF)
            top = dot(w00, wide[:HALF], NN)
            low = dot(jnp.concatenate([w10, w11], axis=1), wide, NN)
            n_ref[base : base + HALF, col] = top[:, :DH]
            d_ref[base : base + HALF, col] = top[:, DH:]
            n_ref[base + HALF : base + BLOCK, col] = low[:, :DH]
            d_ref[base + HALF : base + BLOCK, col] = low[:, DH:]


def inside(q, fk, v, chunk, after):
    shape = (2 * BLOCK, NH * DH)
    return call(
        functools.partial(inside_kernel, chunk),
        "inside",
        (q, fk, v),
        [(shape, BF), (shape, F32), (shape, F32)],
        after,
    )


def attend_kernel(chunk, f_ref, n_ref, d_ref, loc_ref, mine, back, a0, a1, r_ref):
    _, core, _, _ = place()
    for block, a_ref in enumerate((a0, a1)):
        row = rows_of(block)
        for head in range(NH):
            col = cols(head)
            fq = f_ref[row, col]
            state = whole(core, (mine, back), head) + loc_ref[2 * chunk + block, head]
            both = jnp.concatenate(
                [state[:DH], jnp.broadcast_to(state[DH : DH + 1], (DH, DH))], axis=0
            )
            sums = jnp.concatenate(halves(both), axis=1)
            past = dot(jnp.concatenate([fq, fq], axis=1), sums, NT)
            inv = 1.0 / (past[:, DH:] + d_ref[row, col])
            r_ref[row, col] = inv
            a_ref[:, col] = ((past[:, :DH] + n_ref[row, col]) * inv).astype(BF)


def attend(near, loc, prior, chunk, after):
    return call(
        functools.partial(attend_kernel, chunk),
        "attend",
        (*near, loc, *prior),
        [((BLOCK, NH * DH), BF)] * 2 + [((2 * BLOCK, NH * DH), F32)],
        after,
    )


def project_kernel(
    dims, xa, xb, ga, gb, wh, wx, wd, am, ao, bm, bo, keep_a, keep_b, to_x, to_d
):
    _, core, _, _ = place()
    even = core == 0
    a_h = jnp.where(even, am[...], ao[...])
    a_d = jnp.where(even, ao[...], am[...])
    b_h = jnp.where(even, bm[...], bo[...])
    b_x = jnp.where(even, bo[...], bm[...])
    if dims == NT:
        ka, sa, kb, sb = wx[...], (b_h, b_x), wd[...], (a_h, a_d)
    else:
        ka, sa, kb, sb = a_h, (wd[...], a_d), b_h, (wx[...], b_x)
    to_d[...] = (dot(xa[...], sa[0], dims) + dot(ga[...], sa[1], dims)).astype(BF)
    to_x[...] = (dot(xb[...], sb[0], dims) + dot(gb[...], sb[1], dims)).astype(BF)
    keep_a[...] = dot(xa[...], wh[...], dims) + dot(ga[...], ka, dims)
    keep_b[...] = dot(xb[...], wh[...], dims) + dot(gb[...], kb, dims)


def project(dims, xa, xb, ga, gb, weights, after):
    shape = (BLOCK, NH * DH)
    return call(
        functools.partial(project_kernel, dims),
        "project",
        (xa, xb, ga, gb, *weights),
        [(shape, F32)] * 2 + [(shape, BF)] * 2,
        after,
    )


def finish_kernel(chunk, ka, kb, ga, gb, *rest):
    for block, (keep, got) in enumerate(((ka, ga), (kb, gb))):
        rest[-1][rows_of(2 * chunk + block)] = (keep[...] + got[...].astype(F32)).astype(BF)


def finish(keep, got, chunk, before):
    return call(
        functools.partial(finish_kernel, chunk),
        "finish",
        (*keep, *got, *before),
        [((NB * BLOCK, NH * DH), BF)],
        aliases={4: 0} if before else None,
    )[0]


def numden_kernel(f_ref, r_ref, a0, a1, k0, k1, p0, p1, *rest):
    first = len(rest) == 4
    gn_ref, den_ref, sum_ref, tot_ref = rest if first else rest[1:5]
    lane = lax.broadcasted_iota(jnp.int32, (BLOCK, DH), 1)
    totals_ = [None if first else rest[0][head] for head in range(NH)]
    for block, (a_ref, k_ref, p_ref) in enumerate(((a0, k0, p0), (a1, k1, p1))):
        row = rows_of(block)
        dens = jnp.zeros((BLOCK, DH), BF)
        for head in range(NH):
            col = cols(head)
            fq = f_ref[row, col]
            grad = k_ref[:, col] + p_ref[:, col].astype(F32)
            inv = r_ref[row, col]
            num = (grad * inv).astype(BF)
            gn_ref[row, col] = num
            den = -jnp.sum(grad * a_ref[:, col].astype(F32), axis=1, keepdims=True) * inv
            upper = den.astype(BF)
            lower = (den - upper.astype(F32)).astype(BF)
            dens = jnp.where(lane == 2 * head, upper, dens)
            dens = jnp.where(lane == 2 * head + 1, lower, dens)
            sums = with_row(
                dot(num, fq, TN), jnp.sum(den * fq.astype(F32), axis=0, keepdims=True)
            )
            sum_ref[block, head] = sums
            before = totals_[head]
            totals_[head] = sums if before is None else before + sums
        den_ref[row] = dens
    if first:
        for head in range(NH):
            tot_ref[head] = totals_[head]
    else:
        split(place()[1], totals_, tot_ref, rest[5])


def numden(f, r, a, keep, got, before, after):
    return call(
        numden_kernel,
        "numden",
        (f, r, *a, *keep, *got, *before),
        [
            ((2 * BLOCK, NH * DH), BF),
            ((2 * BLOCK, DH), BF),
            ((2, NH, ROWS, DH), F32),
            *([(HALF_STATE, F32)] * 2 if before else [((NH, ROWS, DH), F32)]),
        ],
        after,
    )


def local_kernel(
    block, f_ref, k_ref, v_ref, n_ref, d_ref, loc_ref, mine, back, *rest
):
    gq_ref, gk_ref, gv_ref = rest[-3:]
    _, core, _, _ = place()
    causal = lax.broadcasted_iota(jnp.int32, (HALF, HALF), 0) <= lax.broadcasted_iota(
        jnp.int32, (HALF, HALF), 1
    )
    lane = lax.broadcasted_iota(jnp.int32, (BLOCK, DH), 1)
    top, low = slice(0, HALF), slice(HALF, BLOCK)
    near, row = rows_of(block % 2), rows_of(block)
    dens = d_ref[near]
    for head in range(NH):
        col = cols(head)
        fq = f_ref[near, col]
        fk = k_ref[row, col]
        num = n_ref[near, col]
        pick = ((lane == 2 * head) | (lane == 2 * head + 1)).astype(F32).astype(BF)
        left = jnp.concatenate([v_ref[row, col], pick], axis=1)
        right = jnp.concatenate([num, dens], axis=1)

        def pair(a, b, s, t, mask):
            out = dot(a[s], b[t], NT)
            return (jnp.where(causal, out, 0.0) if mask else out).astype(BF)

        w00 = pair(fk, fq, top, top, True)
        w01 = pair(fk, fq, top, low, False)
        w11 = pair(fk, fq, low, low, True)
        g00 = pair(left, right, top, top, True)
        g01 = pair(left, right, top, low, False)
        g11 = pair(left, right, low, low, True)
        gv_ref[top, col] = dot(jnp.concatenate([w00, w01], axis=1), num, NN)
        gv_ref[low, col] = dot(w11, num[low], NN)
        gk_ref[top, col] = dot(jnp.concatenate([g00, g01], axis=1), fq, NN)
        gk_ref[low, col] = dot(g11, fq[low], NN)
        state = whole(core, (mine, back), head) + loc_ref[block, head]
        past = dot(
            jnp.concatenate([num, num], axis=1),
            jnp.concatenate(halves(state[:DH]), axis=0),
            NN,
        )
        den = dens[:, 2 * head : 2 * head + 1].astype(F32) + dens[
            :, 2 * head + 1 : 2 * head + 2
        ].astype(F32)
        past = past + den * state[DH : DH + 1]
        tilt = jnp.minimum(fq.astype(F32), 1.0)
        gq_ref[row.start : row.start + HALF, col] = (tilt[top] * (past[top] + dot(g00, fk[top], TN))).astype(BF)
        gq_ref[row.start + HALF : row.stop, col] = (
            tilt[low]
            * (past[low] + dot(jnp.concatenate([g01, g11], axis=0), fk, TN))
        ).astype(BF)


def local(f, fk, v, num, den, loc, prior, block, before, after):
    shape = (BLOCK, NH * DH)
    return call(
        functools.partial(local_kernel, block),
        "local",
        (f, fk, v, num, den, loc, *prior, *before),
        [((NB * BLOCK, NH * DH), BF), (shape, F32), (shape, F32)],
        after,
        aliases={8: 0} if before else None,
    )


def later_kernel(k_ref, v_ref, *rest):
    near, (s0_ref, s1_ref, mine, back, gk_ref, gv_ref) = rest[:8], rest[8:]
    _, core, _, _ = place()
    for head in range(NH):
        col = cols(head)
        state = whole(core, (mine, back), head)
        for block in reversed(range(NB)):
            row = rows_of(block)
            fk = k_ref[row, col]
            val = v_ref[row, col]
            upper, lower = halves(state[:DH])
            gk = near[2 * block][:, col] + dot(
                jnp.concatenate([val, val], axis=1),
                jnp.concatenate([upper, lower], axis=0),
                NN,
            )
            gk = gk + state[DH : DH + 1]
            gk_ref[row, col] = (jnp.minimum(fk.astype(F32), 1.0) * gk).astype(BF)
            gv = near[2 * block + 1][:, col] + dot(
                jnp.concatenate([fk, fk], axis=1),
                jnp.concatenate([upper, lower], axis=1),
                NT,
            )
            gv_ref[row, col] = gv.astype(BF)
            if block:
                state = state + (s0_ref, s1_ref)[block // 2][block % 2, head]


def later(fk, v, near, s0, s1, behind, after):
    return call(
        later_kernel,
        "later",
        (fk, v, *near, s0, s1, *behind),
        [((NB * BLOCK, NH * DH), BF)] * 2,
        after,
    )


A_PAIRS = [(h, h ^ 1) for h in range(4)]
B_PAIRS = [(h, 3 - h) for h in range(4)]


def ctx_pairs(change):
    out = []
    for y in range(4):
        for z in range(4):
            for c in range(2):
                y2, z2, c2 = change(y, z, c)
                out.append((y * 8 + z * 2 + c, y2 * 8 + z2 * 2 + c2))
    return out


def swap(x, change):
    return lax.ppermute(x, "ctx", ctx_pairs(change))


def sibling(x):
    return swap(x, lambda y, z, c: (y, z, 1 - c))


def flags(reverse):
    _, core, z, y = place()
    if reverse:
        return core == 0, z % 2 == 0, z < 2, y % 2 == 0, y < 2
    return core == 1, z % 2 == 1, z >= 2, y % 2 == 1, y >= 2


def add_kernel(a_ref, b_ref, out_ref):
    out_ref[...] = a_ref[...] + b_ref[...]


def column_kernel(reverse, chip, near, far, both):
    _, _, _, odd, high = flags(reverse)
    both[0] = jnp.where(odd, near[...], 0.0) + jnp.where(high, far[...], 0.0)
    both[1] = chip[...]


def row_kernel(reverse, own, got, message, partial):
    _, odd, high, _, _ = flags(reverse)
    column = own[0] + got[0]
    message[...] = column + jnp.where(high, 0.0, own[1] + got[1])
    partial[...] = column + jnp.where(odd, got[1], 0.0)


def last_kernel(reverse, partial, more, mine, got, my, its):
    second, _, _, _, _ = flags(reverse)
    ahead = partial[...] + more[...]
    my[...] = ahead + jnp.where(second, got[...], 0.0)
    its[...] = ahead + jnp.where(second, 0.0, mine[...])


def entering(mine, other, reverse):
    one = [(HALF_STATE, F32)]
    got = yield other, lambda y, z, c: (y, z, 1 - c)
    (chip,) = call(add_kernel, "chip", (mine, got), one)
    near = yield chip, lambda y, z, c: (y ^ 1, z, c)
    (pair,) = call(add_kernel, "pair", (chip, near), one)
    far = yield pair, lambda y, z, c: (3 - y, z, c)
    (both,) = call(
        functools.partial(column_kernel, reverse),
        "column",
        (chip, near, far),
        [((2, *HALF_STATE), F32)],
    )
    swapped = yield both, lambda y, z, c: (y, z ^ 1, c)
    message, partial = call(
        functools.partial(row_kernel, reverse), "row", (both, swapped), one * 2
    )
    more = yield message, lambda y, z, c: (y, 3 - z, c)
    my, its = call(
        functools.partial(last_kernel, reverse), "last", (partial, more, mine, got), one * 2
    )
    back = yield its, lambda y, z, c: (y, z, 1 - c)
    yield (my, back), None


class Scan:
    def __init__(self, mine, other, reverse):
        self.steps = entering(mine, other, reverse)
        self.message, self.move = next(self.steps)

    def hop(self, *after):
        sent = tie(self.message, *after)
        self.message, self.move = self.steps.send(swap(sent, self.move))
        return sent


def on_device(queries, key_input, value_input, out_weight, cotangent):
    def to_x(x):
        return lax.ppermute(x, "head", A_PAIRS)

    def to_d(x):
        return lax.ppermute(x, "head", B_PAIRS)

    piece = ((BLOCK, NH * DH), BF)
    a_send, b_send, block0, block1 = stage(
        first_pieces, "first", (out_weight, cotangent), [piece] * 4
    )
    block2, block3, *own = stage(
        second_pieces, "second", (out_weight, cotangent), [piece] * 5, (a_send,)
    )
    blocks = (block0, block1, block2, block3)
    a_mine, b_mine = to_x(a_send), to_d(b_send)
    cots = [(to_x(block0), to_d(block1)), (to_x(block2), to_d(block3))]

    loc, fk, mine, other = totals(key_input, value_input, (block2,))
    scan = Scan(mine, other, False)
    scan.hop()
    sent = scan.hop()
    near0 = inside(queries, fk, value_input, 0, (sent,))
    sent = scan.hop(near0[0])
    weights = (*own, a_mine, sibling(a_mine), b_mine, sibling(b_mine))
    near1 = inside(queries, fk, value_input, 1, (sent,))
    near = (near0, near1)
    sent = scan.hop(near1[0])

    def grad_project(c, after):
        keep_a, keep_b, send_x, send_d = project(
            NT, blocks[2 * c], blocks[2 * c + 1], *cots[c], weights, after
        )
        return (keep_a, keep_b), (to_d(send_d), to_x(send_x))

    grads = [grad_project(0, (sent,)), None]
    scan.hop(grads[0][0][0])
    scan.hop()
    prior = scan.message
    heads = [attend(near[0], loc, prior, 0, ())]
    grads[1] = grad_project(1, (heads[0][0],))
    heads.append(attend(near[1], loc, prior, 1, (grads[1][0][0],)))
    gathered = [(to_x(heads[c][0]), to_d(heads[c][1])) for c in range(2)]

    nums = []
    for c in range(2):
        before = (nums[0][3],) if c else ()
        nums.append(numden(near[c][0], heads[c][2], heads[c][:2], *grads[c], before, ()))
    scan = Scan(*nums[1][3:], True)

    def out_project(c, after):
        keep_a, keep_b, send_x, send_d = project(
            NN, *heads[c][:2], *gathered[c], weights, after
        )
        return (keep_a, keep_b), (to_d(send_d), to_x(send_x))

    parts = []

    def local_block(block, after):
        c = block // 2
        before = (parts[-1][0],) if parts else ()
        parts.append(
            local(
                near[c][0],
                fk,
                value_input,
                *nums[c][:2],
                loc,
                prior,
                block,
                before,
                after,
            )
        )
        return parts[-1][1]

    sent = scan.hop()
    done = local_block(0, (sent,))
    sent = scan.hop(done)
    done = local_block(1, (sent,))
    sent = scan.hop(done)
    out0 = out_project(0, (sent,))
    sent = scan.hop(out0[0][0])
    done = local_block(2, (sent, out0[0][0]))
    sent = scan.hop(done)
    out1 = out_project(1, (sent,))
    sent = scan.hop(out1[0][0])
    done = local_block(3, (sent, out1[0][0]))
    half = finish(*out0, 0, ())
    grad_key, grad_value = later(
        fk,
        value_input,
        [x for part in parts for x in part[1:]],
        nums[0][2],
        nums[1][2],
        scan.message,
        (),
    )
    return (finish(*out1, 1, (half,)), parts[-1][0], grad_key, grad_value)


def solution(mesh):
    in_specs = (
        P("ctx", "head"),
        P("ctx", "head"),
        P("ctx", "head"),
        P("head", None),
        P("ctx", "head"),
    )
    out_specs = (P("ctx", "head"), P("ctx", "head"), P("ctx", "head"), P("ctx", "head"))
    return jax.shard_map(
        on_device, mesh=mesh, in_specs=in_specs, out_specs=out_specs, check_vma=False
    )
```

```python
import functools

import jax
import jax.numpy as jnp
from jax import lax
from jax.experimental import pallas as pl
from jax.experimental.pallas import tpu as pltpu
from jax.sharding import PartitionSpec as P

DH = 128
BLOCK = 512
HALF = BLOCK // 2
NH = 4
NB = 4
ROWS = DH + 8
BF = jnp.bfloat16
F32 = jnp.float32

PARAMS = pltpu.CompilerParams(vmem_limit_bytes=14 * 1024 * 1024)
VMEM = pl.BlockSpec(memory_space=pltpu.VMEM)
HBM = pl.BlockSpec(memory_space=pltpu.HBM)

NN = (((1,), (0,)), ((), ()))
NT = (((1,), (1,)), ((), ()))
TN = (((0,), (0,)), ((), ()))


def dot(a, b, dims):
    return lax.dot_general(a, b, dims, preferred_element_type=F32)


def feature(lifted):
    return jnp.where(lifted > 0, lifted + 1.0, jnp.exp(jnp.minimum(lifted, 0.0)))


def slope(lifted):
    return jnp.where(lifted > 0, 1.0, jnp.exp(jnp.minimum(lifted, 0.0)))


def halves(state):
    upper = state.astype(BF)
    return upper, (state - upper.astype(F32)).astype(BF)


def call(kernel, name, args, outs, after=(), aliases=None):
    count, extra = len(args), len(after)

    def body(*refs):
        kernel(*refs[:count], *refs[count + extra :])

    return pl.pallas_call(
        body,
        in_specs=[VMEM] * (count + extra),
        out_specs=[VMEM] * len(outs),
        out_shape=[pltpu.VMEM(shape, dtype) for shape, dtype in outs],
        input_output_aliases=aliases or {},
        compiler_params=PARAMS,
        name=name,
    )(*args, *after)


def place():
    head, index = lax.axis_index("head"), lax.axis_index("ctx")
    return head, index % 2, (index // 2) % 4, index // 8


def partner(head):
    return head + 1 - 2 * (head % 2)


def tie(x, *after):
    return lax.optimization_barrier((x, *after))[0] if after else x


def cols(head):
    return slice(head * DH, (head + 1) * DH)


def rows_of(block):
    return slice(block * BLOCK, (block + 1) * BLOCK)


def with_row(state, row):
    return jnp.concatenate([state, jnp.broadcast_to(row, (ROWS - DH, DH))], axis=0)


def stage(kernel, name, args, outs, after=()):
    args = tuple(pltpu.with_memory_space_constraint(x, pltpu.HBM) for x in args)
    count, extra = len(args), len(after)

    def body(*refs):
        sems = refs[-1]
        copies = [
            pltpu.make_async_copy(source, target, sems.at[i])
            for i, (source, target) in enumerate(
                zip(kernel(*refs[:count]), refs[count + extra : -1])
            )
        ]
        for copy in copies:
            copy.start()
        for copy in copies:
            copy.wait()

    return pl.pallas_call(
        body,
        in_specs=[HBM] * count + [VMEM] * extra,
        out_specs=[VMEM] * len(outs),
        out_shape=[pltpu.VMEM(shape, dtype) for shape, dtype in outs],
        scratch_shapes=[pltpu.SemaphoreType.DMA((len(outs),))],
        compiler_params=PARAMS,
        name=name,
    )(*args, *after)


def quarter(w_ref, index, rows=slice(None)):
    size = NH * DH
    return w_ref.at[rows, pl.ds(pl.multiple_of(index * size, size), size)]


def half_rows(which):
    return pl.ds(pl.multiple_of(which * HALF, HALF), HALF)


def first_pieces(w_ref, c_ref):
    head, core, z, y = place()
    x, d = partner(head), 3 - head
    return (
        quarter(w_ref, x + core * (3 - 2 * x), half_rows(y % 2)),
        quarter(w_ref, d + core * (partner(d) - d), half_rows(z % 2)),
        c_ref.at[rows_of(0)],
        c_ref.at[rows_of(1)],
    )


def second_pieces(w_ref, c_ref):
    head, _, _, _ = place()
    return (
        c_ref.at[rows_of(2)],
        c_ref.at[rows_of(3)],
        quarter(w_ref, head),
        quarter(w_ref, partner(head)),
        quarter(w_ref, 3 - head),
    )


def assemble_kernel(a_own, a_got, b_own, b_got, out_ref):
    _, _, z, y = place()
    out_ref[0, half_rows(y % 2)] = a_own[...]
    out_ref[0, half_rows(1 - y % 2)] = a_got[...]
    out_ref[1, half_rows(z % 2)] = b_own[...]
    out_ref[1, half_rows(1 - z % 2)] = b_got[...]


HALF_STATE = (NH // 2, ROWS, DH)


def split(core, sums, mine_ref, other_ref):
    for i in range(NH // 2):
        low, high = sums[i], sums[NH // 2 + i]
        mine_ref[i] = jnp.where(core == 0, low, high)
        other_ref[i] = jnp.where(core == 0, high, low)


def whole(core, pair, head):
    mine, back = pair
    slot = head % (NH // 2)
    return jnp.where(core == head // (NH // 2), mine[slot], back[slot])


def totals_kernel(k_ref, v_ref, loc_ref, fk_ref, mine_ref, other_ref):
    _, core, _, _ = place()
    sums = []
    for head in range(NH):
        col = cols(head)
        total = jnp.zeros((ROWS, DH), F32)
        for block in range(NB):
            row = rows_of(block)
            feat = feature(k_ref[row, col].astype(F32)).astype(BF)
            fk_ref[row, col] = feat
            loc_ref[block, head] = total
            total = total + with_row(
                dot(v_ref[row, col], feat, TN),
                jnp.sum(feat.astype(F32), axis=0, keepdims=True),
            )
        sums.append(total)
    split(core, sums, mine_ref, other_ref)


def totals(k, v, after):
    return call(
        totals_kernel,
        "totals",
        (k, v),
        [((NB, NH, ROWS, DH), F32), ((NB * BLOCK, NH * DH), BF), (HALF_STATE, F32), (HALF_STATE, F32)],
        after,
    )


def inside_kernel(chunk, q_ref, k_ref, v_ref, f_ref, n_ref, d_ref):
    lower = lax.broadcasted_iota(jnp.int32, (HALF, HALF), 0) >= lax.broadcasted_iota(
        jnp.int32, (HALF, HALF), 1
    )
    ones = jnp.ones((BLOCK, DH), BF)
    for block in range(2):
        row = rows_of(2 * chunk + block)
        base = block * BLOCK
        for head in range(NH):
            col = cols(head)
            fq = feature(q_ref[row, col].astype(F32)).astype(BF)
            f_ref[base : base + BLOCK, col] = fq
            fk = k_ref[row, col]
            wide = jnp.concatenate([v_ref[row, col], ones], axis=1)
            w00 = jnp.where(lower, dot(fq[:HALF], fk[:HALF], NT), 0.0).astype(BF)
            w10 = dot(fq[HALF:], fk[:HALF], NT).astype(BF)
            w11 = jnp.where(lower, dot(fq[HALF:], fk[HALF:], NT), 0.0).astype(BF)
            top = dot(w00, wide[:HALF], NN)
            low = dot(jnp.concatenate([w10, w11], axis=1), wide, NN)
            n_ref[base : base + HALF, col] = top[:, :DH]
            d_ref[base : base + HALF, col] = top[:, DH:]
            n_ref[base + HALF : base + BLOCK, col] = low[:, :DH]
            d_ref[base + HALF : base + BLOCK, col] = low[:, DH:]


def inside(q, fk, v, chunk, after):
    shape = (2 * BLOCK, NH * DH)
    return call(
        functools.partial(inside_kernel, chunk),
        "inside",
        (q, fk, v),
        [(shape, BF), (shape, F32), (shape, F32)],
        after,
    )


def attend_kernel(chunk, f_ref, n_ref, d_ref, loc_ref, mine, back, a0, a1, r_ref):
    _, core, _, _ = place()
    for block, a_ref in enumerate((a0, a1)):
        row = rows_of(block)
        for head in range(NH):
            col = cols(head)
            fq = f_ref[row, col]
            state = whole(core, (mine, back), head) + loc_ref[2 * chunk + block, head]
            both = jnp.concatenate(
                [state[:DH], jnp.broadcast_to(state[DH : DH + 1], (DH, DH))], axis=0
            )
            sums = jnp.concatenate(halves(both), axis=1)
            past = dot(jnp.concatenate([fq, fq], axis=1), sums, NT)
            inv = 1.0 / (past[:, DH:] + d_ref[row, col])
            r_ref[row, col] = inv
            a_ref[:, col] = ((past[:, :DH] + n_ref[row, col]) * inv).astype(BF)


def attend(near, loc, prior, chunk, after):
    return call(
        functools.partial(attend_kernel, chunk),
        "attend",
        (*near, loc, *prior),
        [((BLOCK, NH * DH), BF)] * 2 + [((2 * BLOCK, NH * DH), F32)],
        after,
    )


def project_kernel(
    dims, xa, xb, ga, gb, wh, wx, wd, mine, other, keep_a, keep_b, to_x, to_d
):
    _, core, _, _ = place()
    even = core == 0
    a_h = jnp.where(even, mine[0], other[0])
    a_d = jnp.where(even, other[0], mine[0])
    b_h = jnp.where(even, mine[1], other[1])
    b_x = jnp.where(even, other[1], mine[1])
    if dims == NT:
        ka, sa, kb, sb = wx[...], (b_h, b_x), wd[...], (a_h, a_d)
    else:
        ka, sa, kb, sb = a_h, (wd[...], a_d), b_h, (wx[...], b_x)
    to_d[...] = (dot(xa[...], sa[0], dims) + dot(ga[...], sa[1], dims)).astype(BF)
    to_x[...] = (dot(xb[...], sb[0], dims) + dot(gb[...], sb[1], dims)).astype(BF)
    keep_a[...] = dot(xa[...], wh[...], dims) + dot(ga[...], ka, dims)
    keep_b[...] = dot(xb[...], wh[...], dims) + dot(gb[...], kb, dims)


def project(dims, xa, xb, ga, gb, weights, after):
    shape = (BLOCK, NH * DH)
    return call(
        functools.partial(project_kernel, dims),
        "project",
        (xa, xb, ga, gb, *weights),
        [(shape, F32)] * 2 + [(shape, BF)] * 2,
        after,
    )


def finish_kernel(ka, kb, ga, gb, whole_ref, out_ref, rows_ref, sem):
    del whole_ref
    copies = []
    for block, (keep, got) in enumerate(((ka, ga), (kb, gb))):
        row = rows_of(block)
        rows_ref[row] = (keep[...] + got[...].astype(F32)).astype(BF)
        copies.append(
            pltpu.make_async_copy(
                rows_ref.at[row], out_ref.at[rows_of(2 + block)], sem.at[block]
            )
        )
        copies[-1].start()
    for copy in copies:
        copy.wait()


def finish(keep, got, whole_out):
    return pl.pallas_call(
        finish_kernel,
        in_specs=[VMEM] * 4 + [HBM],
        out_specs=HBM,
        out_shape=jax.ShapeDtypeStruct((NB * BLOCK, NH * DH), BF),
        scratch_shapes=[
            pltpu.VMEM((2 * BLOCK, NH * DH), BF),
            pltpu.SemaphoreType.DMA((2,)),
        ],
        input_output_aliases={4: 0},
        compiler_params=PARAMS,
        name="finish",
    )(*keep, *got, whole_out)


def numden_kernel(f_ref, r_ref, a0, a1, k0, k1, p0, p1, *rest):
    first = len(rest) == 4
    gn_ref, den_ref, sum_ref, tot_ref = rest if first else rest[1:5]
    lane = lax.broadcasted_iota(jnp.int32, (BLOCK, DH), 1)
    totals_ = [None if first else rest[0][head] for head in range(NH)]
    for block, (a_ref, k_ref, p_ref) in enumerate(((a0, k0, p0), (a1, k1, p1))):
        row = rows_of(block)
        dens = jnp.zeros((BLOCK, DH), BF)
        for head in range(NH):
            col = cols(head)
            fq = f_ref[row, col]
            grad = k_ref[:, col] + p_ref[:, col].astype(F32)
            inv = r_ref[row, col]
            num = (grad * inv).astype(BF)
            gn_ref[row, col] = num
            den = -jnp.sum(grad * a_ref[:, col].astype(F32), axis=1, keepdims=True) * inv
            upper = den.astype(BF)
            lower = (den - upper.astype(F32)).astype(BF)
            dens = jnp.where(lane == 2 * head, upper, dens)
            dens = jnp.where(lane == 2 * head + 1, lower, dens)
            sums = with_row(
                dot(num, fq, TN), jnp.sum(den * fq.astype(F32), axis=0, keepdims=True)
            )
            sum_ref[block, head] = sums
            before = totals_[head]
            totals_[head] = sums if before is None else before + sums
        den_ref[row] = dens
    if first:
        for head in range(NH):
            tot_ref[head] = totals_[head]
    else:
        split(place()[1], totals_, tot_ref, rest[5])


def numden(f, r, a, keep, got, before, after):
    return call(
        numden_kernel,
        "numden",
        (f, r, *a, *keep, *got, *before),
        [
            ((2 * BLOCK, NH * DH), BF),
            ((2 * BLOCK, DH), BF),
            ((2, NH, ROWS, DH), F32),
            *([(HALF_STATE, F32)] * 2 if before else [((NH, ROWS, DH), F32)]),
        ],
        after,
    )


def local_kernel(
    block, f_ref, k_ref, v_ref, n_ref, d_ref, loc_ref, mine, back, *rest
):
    gq_ref, gk_ref, gv_ref = rest[-3:]
    _, core, _, _ = place()
    causal = lax.broadcasted_iota(jnp.int32, (HALF, HALF), 0) <= lax.broadcasted_iota(
        jnp.int32, (HALF, HALF), 1
    )
    lane = lax.broadcasted_iota(jnp.int32, (BLOCK, DH), 1)
    top, low = slice(0, HALF), slice(HALF, BLOCK)
    near, row = rows_of(block % 2), rows_of(block)
    dens = d_ref[near]
    for head in range(NH):
        col = cols(head)
        fq = f_ref[near, col]
        fk = k_ref[row, col]
        num = n_ref[near, col]
        pick = ((lane == 2 * head) | (lane == 2 * head + 1)).astype(F32).astype(BF)
        left = jnp.concatenate([v_ref[row, col], pick], axis=1)
        right = jnp.concatenate([num, dens], axis=1)

        def pair(a, b, s, t, mask):
            out = dot(a[s], b[t], NT)
            return (jnp.where(causal, out, 0.0) if mask else out).astype(BF)

        w00 = pair(fk, fq, top, top, True)
        w01 = pair(fk, fq, top, low, False)
        w11 = pair(fk, fq, low, low, True)
        g00 = pair(left, right, top, top, True)
        g01 = pair(left, right, top, low, False)
        g11 = pair(left, right, low, low, True)
        gv_ref[top, col] = dot(jnp.concatenate([w00, w01], axis=1), num, NN)
        gv_ref[low, col] = dot(w11, num[low], NN)
        gk_ref[top, col] = dot(jnp.concatenate([g00, g01], axis=1), fq, NN)
        gk_ref[low, col] = dot(g11, fq[low], NN)
        state = whole(core, (mine, back), head) + loc_ref[block, head]
        past = dot(
            jnp.concatenate([num, num], axis=1),
            jnp.concatenate(halves(state[:DH]), axis=0),
            NN,
        )
        den = dens[:, 2 * head : 2 * head + 1].astype(F32) + dens[
            :, 2 * head + 1 : 2 * head + 2
        ].astype(F32)
        past = past + den * state[DH : DH + 1]
        tilt = jnp.minimum(fq.astype(F32), 1.0)
        gq_ref[row.start : row.start + HALF, col] = (tilt[top] * (past[top] + dot(g00, fk[top], TN))).astype(BF)
        gq_ref[row.start + HALF : row.stop, col] = (
            tilt[low]
            * (past[low] + dot(jnp.concatenate([g01, g11], axis=0), fk, TN))
        ).astype(BF)


def local(f, fk, v, num, den, loc, prior, block, before, after):
    shape = (BLOCK, NH * DH)
    return call(
        functools.partial(local_kernel, block),
        "local",
        (f, fk, v, num, den, loc, *prior, *before),
        [((NB * BLOCK, NH * DH), BF), (shape, F32), (shape, F32)],
        after,
        aliases={8: 0} if before else None,
    )


def later_kernel(k_ref, v_ref, gq_ref, ka, kb, ga, gb, *rest):
    near, (s0_ref, s1_ref, mine, back) = rest[:8], rest[8:12]
    out_hbm, gq_hbm, gk_hbm, gv_hbm, out_ref, gk_ref, gv_ref, sems = rest[12:]
    _, core, _, _ = place()
    copies = []

    def send(source, target):
        copies.append(pltpu.make_async_copy(source, target, sems.at[len(copies)]))
        copies[-1].start()

    send(gq_ref, gq_hbm)
    for block, (keep, got) in enumerate(((ka, ga), (kb, gb))):
        row = rows_of(block)
        out_ref[row] = (keep[...] + got[...].astype(F32)).astype(BF)
        send(out_ref.at[row], out_hbm.at[row])
    states = [whole(core, (mine, back), head) for head in range(NH)]
    for block in reversed(range(NB)):
        row = rows_of(block)
        for head in range(NH):
            col = cols(head)
            fk = k_ref[row, col]
            val = v_ref[row, col]
            upper, lower = halves(states[head][:DH])
            gk = near[2 * block][:, col] + dot(
                jnp.concatenate([val, val], axis=1),
                jnp.concatenate([upper, lower], axis=0),
                NN,
            )
            gk = gk + states[head][DH : DH + 1]
            gk_ref[row, col] = (jnp.minimum(fk.astype(F32), 1.0) * gk).astype(BF)
            gv = near[2 * block + 1][:, col] + dot(
                jnp.concatenate([fk, fk], axis=1),
                jnp.concatenate([upper, lower], axis=1),
                NT,
            )
            gv_ref[row, col] = gv.astype(BF)
            if block:
                states[head] = states[head] + (s0_ref, s1_ref)[block // 2][block % 2, head]
        send(gk_ref.at[row], gk_hbm.at[row])
        send(gv_ref.at[row], gv_hbm.at[row])
    for copy in copies:
        copy.wait()


def later(fk, v, gq, keep, got, near, s0, s1, behind):
    full = (NB * BLOCK, NH * DH)
    args = (fk, v, gq, *keep, *got, *near, s0, s1, *behind)
    return pl.pallas_call(
        later_kernel,
        in_specs=[VMEM] * len(args),
        out_specs=[HBM] * 4,
        out_shape=[jax.ShapeDtypeStruct(full, BF)] * 4,
        scratch_shapes=[
            pltpu.VMEM((2 * BLOCK, NH * DH), BF),
            pltpu.VMEM(full, BF),
            pltpu.VMEM(full, BF),
            pltpu.SemaphoreType.DMA((3 + 2 * NB,)),
        ],
        compiler_params=PARAMS,
        name="later",
    )(*args)


A_PAIRS = [(h, h ^ 1) for h in range(4)]
B_PAIRS = [(h, 3 - h) for h in range(4)]


def ctx_pairs(change):
    out = []
    for y in range(4):
        for z in range(4):
            for c in range(2):
                y2, z2, c2 = change(y, z, c)
                out.append((y * 8 + z * 2 + c, y2 * 8 + z2 * 2 + c2))
    return out


def swap(x, change):
    return lax.ppermute(x, "ctx", ctx_pairs(change))


def sibling(x):
    return swap(x, lambda y, z, c: (y, z, 1 - c))


def flags(reverse):
    _, core, z, y = place()
    if reverse:
        return core == 0, z % 2 == 0, z < 2, y % 2 == 0, y < 2
    return core == 1, z % 2 == 1, z >= 2, y % 2 == 1, y >= 2


def add_kernel(a_ref, b_ref, out_ref):
    out_ref[...] = a_ref[...] + b_ref[...]


def column_kernel(reverse, chip, near, far, both):
    _, _, _, odd, high = flags(reverse)
    both[0] = jnp.where(odd, near[...], 0.0) + jnp.where(high, far[...], 0.0)
    both[1] = chip[...]


def row_kernel(reverse, own, got, message, partial):
    _, odd, high, _, _ = flags(reverse)
    column = own[0] + got[0]
    message[...] = column + jnp.where(high, 0.0, own[1] + got[1])
    partial[...] = column + jnp.where(odd, got[1], 0.0)


def last_kernel(reverse, partial, more, mine, got, my, its):
    second, _, _, _, _ = flags(reverse)
    ahead = partial[...] + more[...]
    my[...] = ahead + jnp.where(second, got[...], 0.0)
    its[...] = ahead + jnp.where(second, 0.0, mine[...])


def entering(mine, other, reverse):
    one = [(HALF_STATE, F32)]
    got = yield other, lambda y, z, c: (y, z, 1 - c)
    (chip,) = call(add_kernel, "chip", (mine, got), one)
    near = yield chip, lambda y, z, c: (y ^ 1, z, c)
    (pair,) = call(add_kernel, "pair", (chip, near), one)
    far = yield pair, lambda y, z, c: (3 - y, z, c)
    (both,) = call(
        functools.partial(column_kernel, reverse),
        "column",
        (chip, near, far),
        [((2, *HALF_STATE), F32)],
    )
    swapped = yield both, lambda y, z, c: (y, z ^ 1, c)
    message, partial = call(
        functools.partial(row_kernel, reverse), "row", (both, swapped), one * 2
    )
    more = yield message, lambda y, z, c: (y, 3 - z, c)
    my, its = call(
        functools.partial(last_kernel, reverse), "last", (partial, more, mine, got), one * 2
    )
    back = yield its, lambda y, z, c: (y, z, 1 - c)
    yield (my, back), None


class Scan:
    def __init__(self, mine, other, reverse):
        self.steps = entering(mine, other, reverse)
        self.message, self.move = next(self.steps)

    def hop(self, *after):
        sent = tie(self.message, *after)
        self.message, self.move = self.steps.send(swap(sent, self.move))
        return sent


def on_device(queries, key_input, value_input, out_weight, cotangent):
    def to_x(x):
        return lax.ppermute(x, "head", A_PAIRS)

    def to_d(x):
        return lax.ppermute(x, "head", B_PAIRS)

    piece = ((BLOCK, NH * DH), BF)
    part = ((HALF, NH * DH), BF)
    a_send, b_send, block0, block1 = stage(
        first_pieces, "first", (out_weight, cotangent), [part, part, piece, piece]
    )
    block2, block3, *own = stage(
        second_pieces, "second", (out_weight, cotangent), [piece] * 5, (a_send,)
    )
    blocks = (block0, block1, block2, block3)
    a_own, b_own = to_x(a_send), to_d(b_send)

    loc, fk, mine, other = totals(key_input, value_input, (block2,))
    cots = [(to_x(tie(block0, mine, a_own)), to_d(tie(block1, mine, b_own)))]
    cots.append((to_x(tie(block2, cots[0][0])), to_d(tie(block3, cots[0][1]))))
    scan = Scan(mine, other, False)
    scan.hop()
    sent = scan.hop()
    a_got = swap(a_own, lambda y, z, c: (y ^ 1, z, c))
    b_got = swap(b_own, lambda y, z, c: (y, z ^ 1, c))
    near0 = inside(queries, fk, value_input, 0, (sent, a_own, b_own, *cots[0]))
    (quarters,) = call(
        assemble_kernel,
        "assemble",
        (a_own, a_got, b_own, b_got),
        [((2, BLOCK, NH * DH), BF)],
        (near0[0],),
    )
    weights = (*own, quarters, sibling(quarters))
    sent = scan.hop(near0[0])
    near = [near0, None]
    sent = scan.hop(quarters)

    def grad_project(c, after):
        keep_a, keep_b, send_x, send_d = project(
            NT, blocks[2 * c], blocks[2 * c + 1], *cots[c], weights, after
        )
        return (keep_a, keep_b), (to_d(send_d), to_x(send_x))

    grads = [grad_project(0, (sent,)), None]
    sent = scan.hop(grads[0][0][0])
    grads[1] = grad_project(1, (sent,))
    sent = scan.hop(grads[1][0][0])
    near[1] = inside(queries, fk, value_input, 1, (sent,))
    prior = scan.message
    heads = [attend(near[0], loc, prior, 0, (near[1][0],))]
    heads.append(attend(near[1], loc, prior, 1, (heads[0][0],)))
    gathered = [(to_x(heads[c][0]), to_d(heads[c][1])) for c in range(2)]

    nums = []
    for c in range(2):
        before = (nums[0][3],) if c else ()
        nums.append(numden(near[c][0], heads[c][2], heads[c][:2], *grads[c], before, ()))
    scan = Scan(*nums[1][3:], True)

    def out_project(c, after):
        keep_a, keep_b, send_x, send_d = project(
            NN, *heads[c][:2], *gathered[c], weights, after
        )
        return (keep_a, keep_b), (to_d(send_d), to_x(send_x))

    parts = []

    def local_block(block, after):
        c = block // 2
        before = (parts[-1][0],) if parts else ()
        parts.append(
            local(
                near[c][0],
                fk,
                value_input,
                *nums[c][:2],
                loc,
                prior,
                block,
                before,
                after,
            )
        )
        return parts[-1][1]

    sent = scan.hop()
    done = local_block(0, (sent,))
    sent = scan.hop(done)
    done = local_block(1, (sent,))
    sent = scan.hop(done)
    out0 = out_project(0, (sent,))
    sent = scan.hop(out0[0][0])
    done = local_block(2, (sent, out0[0][0]))
    sent = scan.hop(done)
    out1 = out_project(1, (sent,))
    sent = scan.hop(out1[0][0])
    done = local_block(3, (sent, out1[0][0]))
    out, grad_query, grad_key, grad_value = later(
        fk,
        value_input,
        parts[-1][0],
        *out0,
        [x for part in parts for x in part[1:]],
        nums[0][2],
        nums[1][2],
        scan.message,
    )
    return finish(*out1, out), grad_query, grad_key, grad_value


def solution(mesh):
    in_specs = (
        P("ctx", "head"),
        P("ctx", "head"),
        P("ctx", "head"),
        P("head", None),
        P("ctx", "head"),
    )
    out_specs = (P("ctx", "head"), P("ctx", "head"), P("ctx", "head"), P("ctx", "head"))
    return jax.shard_map(
        on_device, mesh=mesh, in_specs=in_specs, out_specs=out_specs, check_vma=False
    )
```

```python
import functools

import jax
import jax.numpy as jnp
from jax import lax
from jax.experimental import pallas as pl
from jax.experimental.pallas import tpu as pltpu
from jax.sharding import PartitionSpec as P

DH = 128
BLOCK = 512
HALF = BLOCK // 2
NH = 4
NB = 4
ROWS = DH + 8
BF = jnp.bfloat16
F32 = jnp.float32

PARAMS = pltpu.CompilerParams(vmem_limit_bytes=14 * 1024 * 1024)
VMEM = pl.BlockSpec(memory_space=pltpu.VMEM)
HBM = pl.BlockSpec(memory_space=pltpu.HBM)

NN = (((1,), (0,)), ((), ()))
NT = (((1,), (1,)), ((), ()))
TN = (((0,), (0,)), ((), ()))


def dot(a, b, dims):
    return lax.dot_general(a, b, dims, preferred_element_type=F32)


def feature(lifted):
    return jnp.where(lifted > 0, lifted + 1.0, jnp.exp(jnp.minimum(lifted, 0.0)))


def slope(lifted):
    return jnp.where(lifted > 0, 1.0, jnp.exp(jnp.minimum(lifted, 0.0)))


def halves(state):
    upper = state.astype(BF)
    return upper, (state - upper.astype(F32)).astype(BF)


def call(kernel, name, args, outs, after=(), aliases=None):
    count, extra = len(args), len(after)

    def body(*refs):
        kernel(*refs[:count], *refs[count + extra :])

    return pl.pallas_call(
        body,
        in_specs=[VMEM] * (count + extra),
        out_specs=[VMEM] * len(outs),
        out_shape=[pltpu.VMEM(shape, dtype) for shape, dtype in outs],
        input_output_aliases=aliases or {},
        compiler_params=PARAMS,
        name=name,
    )(*args, *after)


def place():
    head, index = lax.axis_index("head"), lax.axis_index("ctx")
    return head, index % 2, (index // 2) % 4, index // 8


def partner(head):
    return head + 1 - 2 * (head % 2)


def tie(x, *after):
    return lax.optimization_barrier((x, *after))[0] if after else x


def cols(head):
    return slice(head * DH, (head + 1) * DH)


def rows_of(block):
    return slice(block * BLOCK, (block + 1) * BLOCK)


def with_row(state, row):
    return jnp.concatenate([state, jnp.broadcast_to(row, (ROWS - DH, DH))], axis=0)


def stage(kernel, name, args, outs, after=()):
    args = tuple(pltpu.with_memory_space_constraint(x, pltpu.HBM) for x in args)
    count, extra = len(args), len(after)

    def body(*refs):
        sems = refs[-1]
        copies = [
            pltpu.make_async_copy(source, target, sems.at[i])
            for i, (source, target) in enumerate(
                zip(kernel(*refs[:count]), refs[count + extra : -1])
            )
        ]
        for copy in copies:
            copy.start()
        for copy in copies:
            copy.wait()

    return pl.pallas_call(
        body,
        in_specs=[HBM] * count + [VMEM] * extra,
        out_specs=[VMEM] * len(outs),
        out_shape=[pltpu.VMEM(shape, dtype) for shape, dtype in outs],
        scratch_shapes=[pltpu.SemaphoreType.DMA((len(outs),))],
        compiler_params=PARAMS,
        name=name,
    )(*args, *after)


def quarter(w_ref, index, rows=slice(None)):
    size = NH * DH
    return w_ref.at[rows, pl.ds(pl.multiple_of(index * size, size), size)]


def half_rows(which):
    return pl.ds(pl.multiple_of(which * HALF, HALF), HALF)


def first_pieces(w_ref, c_ref):
    head, core, z, y = place()
    x, d = partner(head), 3 - head
    return (
        quarter(w_ref, x + core * (3 - 2 * x), half_rows(y % 2)),
        quarter(w_ref, d + core * (partner(d) - d), half_rows(z % 2)),
        c_ref.at[rows_of(0)],
        c_ref.at[rows_of(1)],
    )


def second_pieces(w_ref, c_ref):
    head, _, _, _ = place()
    return (
        c_ref.at[rows_of(2)],
        c_ref.at[rows_of(3)],
        quarter(w_ref, head),
        quarter(w_ref, partner(head)),
        quarter(w_ref, 3 - head),
    )


def assemble_kernel(a_own, a_got, b_own, b_got, out_ref):
    _, _, z, y = place()
    out_ref[0, half_rows(y % 2)] = a_own[...]
    out_ref[0, half_rows(1 - y % 2)] = a_got[...]
    out_ref[1, half_rows(z % 2)] = b_own[...]
    out_ref[1, half_rows(1 - z % 2)] = b_got[...]


HALF_STATE = (NH // 2, ROWS, DH)


def split(core, sums, mine_ref, other_ref):
    for i in range(NH // 2):
        low, high = sums[i], sums[NH // 2 + i]
        mine_ref[i] = jnp.where(core == 0, low, high)
        other_ref[i] = jnp.where(core == 0, high, low)


def whole(core, pair, head):
    mine, back = pair
    slot = head % (NH // 2)
    return jnp.where(core == head // (NH // 2), mine[slot], back[slot])


def totals_kernel(k_ref, v_ref, loc_ref, fk_ref, mine_ref, other_ref):
    _, core, _, _ = place()
    sums = []
    for head in range(NH):
        col = cols(head)
        total = jnp.zeros((ROWS, DH), F32)
        for block in range(NB):
            row = rows_of(block)
            feat = feature(k_ref[row, col].astype(F32)).astype(BF)
            fk_ref[row, col] = feat
            loc_ref[block, head] = total
            total = total + with_row(
                dot(v_ref[row, col], feat, TN),
                jnp.sum(feat.astype(F32), axis=0, keepdims=True),
            )
        sums.append(total)
    split(core, sums, mine_ref, other_ref)


def totals(k, v, after):
    return call(
        totals_kernel,
        "totals",
        (k, v),
        [((NB, NH, ROWS, DH), F32), ((NB * BLOCK, NH * DH), BF), (HALF_STATE, F32), (HALF_STATE, F32)],
        after,
    )


def inside_kernel(chunk, q_ref, k_ref, v_ref, f_ref, n_ref, d_ref):
    lower = lax.broadcasted_iota(jnp.int32, (HALF, HALF), 0) >= lax.broadcasted_iota(
        jnp.int32, (HALF, HALF), 1
    )
    ones = jnp.ones((BLOCK, DH), BF)
    for block in range(2):
        row = rows_of(2 * chunk + block)
        base = block * BLOCK
        for head in range(NH):
            col = cols(head)
            fq = feature(q_ref[row, col].astype(F32)).astype(BF)
            f_ref[base : base + BLOCK, col] = fq
            fk = k_ref[row, col]
            wide = jnp.concatenate([v_ref[row, col], ones], axis=1)
            w00 = jnp.where(lower, dot(fq[:HALF], fk[:HALF], NT), 0.0).astype(BF)
            w10 = dot(fq[HALF:], fk[:HALF], NT).astype(BF)
            w11 = jnp.where(lower, dot(fq[HALF:], fk[HALF:], NT), 0.0).astype(BF)
            top = dot(w00, wide[:HALF], NN)
            low = dot(jnp.concatenate([w10, w11], axis=1), wide, NN)
            n_ref[base : base + HALF, col] = top[:, :DH]
            d_ref[base : base + HALF, col] = top[:, DH:]
            n_ref[base + HALF : base + BLOCK, col] = low[:, :DH]
            d_ref[base + HALF : base + BLOCK, col] = low[:, DH:]


def inside(q, fk, v, chunk, after):
    shape = (2 * BLOCK, NH * DH)
    return call(
        functools.partial(inside_kernel, chunk),
        "inside",
        (q, fk, v),
        [(shape, BF), (shape, F32), (shape, F32)],
        after,
    )


def attend_kernel(chunk, f_ref, n_ref, d_ref, loc_ref, mine, back, a0, a1, r_ref):
    _, core, _, _ = place()
    for block, a_ref in enumerate((a0, a1)):
        row = rows_of(block)
        for head in range(NH):
            col = cols(head)
            fq = f_ref[row, col]
            state = whole(core, (mine, back), head) + loc_ref[2 * chunk + block, head]
            both = jnp.concatenate(
                [state[:DH], jnp.broadcast_to(state[DH : DH + 1], (DH, DH))], axis=0
            )
            sums = jnp.concatenate(halves(both), axis=1)
            past = dot(jnp.concatenate([fq, fq], axis=1), sums, NT)
            inv = 1.0 / (past[:, DH:] + d_ref[row, col])
            r_ref[row, col] = inv
            a_ref[:, col] = ((past[:, :DH] + n_ref[row, col]) * inv).astype(BF)


def attend(near, loc, prior, chunk, after):
    return call(
        functools.partial(attend_kernel, chunk),
        "attend",
        (*near, loc, *prior),
        [((BLOCK, NH * DH), BF)] * 2 + [((2 * BLOCK, NH * DH), F32)],
        after,
    )


def project_kernel(
    dims, xa, xb, ga, gb, wh, wx, wd, mine, other, keep_a, keep_b, to_x, to_d
):
    _, core, _, _ = place()
    even = core == 0
    a_h = jnp.where(even, mine[0], other[0])
    a_d = jnp.where(even, other[0], mine[0])
    b_h = jnp.where(even, mine[1], other[1])
    b_x = jnp.where(even, other[1], mine[1])
    if dims == NT:
        ka, sa, kb, sb = wx[...], (b_h, b_x), wd[...], (a_h, a_d)
    else:
        ka, sa, kb, sb = a_h, (wd[...], a_d), b_h, (wx[...], b_x)
    to_d[...] = (dot(xa[...], sa[0], dims) + dot(ga[...], sa[1], dims)).astype(BF)
    to_x[...] = (dot(xb[...], sb[0], dims) + dot(gb[...], sb[1], dims)).astype(BF)
    keep_a[...] = dot(xa[...], wh[...], dims) + dot(ga[...], ka, dims)
    keep_b[...] = dot(xb[...], wh[...], dims) + dot(gb[...], kb, dims)


def project(dims, xa, xb, ga, gb, weights, after):
    shape = (BLOCK, NH * DH)
    return call(
        functools.partial(project_kernel, dims),
        "project",
        (xa, xb, ga, gb, *weights),
        [(shape, F32)] * 2 + [(shape, BF)] * 2,
        after,
    )


def finish_kernel(ka, kb, ga, gb, whole_ref, out_ref, rows_ref, sem):
    del whole_ref
    copies = []
    for block, (keep, got) in enumerate(((ka, ga), (kb, gb))):
        row = rows_of(block)
        rows_ref[row] = (keep[...] + got[...].astype(F32)).astype(BF)
        copies.append(
            pltpu.make_async_copy(
                rows_ref.at[row], out_ref.at[rows_of(2 + block)], sem.at[block]
            )
        )
        copies[-1].start()
    for copy in copies:
        copy.wait()


def finish(keep, got, whole_out):
    return pl.pallas_call(
        finish_kernel,
        in_specs=[VMEM] * 4 + [HBM],
        out_specs=HBM,
        out_shape=jax.ShapeDtypeStruct((NB * BLOCK, NH * DH), BF),
        scratch_shapes=[
            pltpu.VMEM((2 * BLOCK, NH * DH), BF),
            pltpu.SemaphoreType.DMA((2,)),
        ],
        input_output_aliases={4: 0},
        compiler_params=PARAMS,
        name="finish",
    )(*keep, *got, whole_out)


def numden_kernel(f_ref, r_ref, a0, a1, k0, k1, p0, p1, *rest):
    first = len(rest) == 4
    gn_ref, den_ref, sum_ref, tot_ref = rest if first else rest[1:5]
    lane = lax.broadcasted_iota(jnp.int32, (BLOCK, DH), 1)
    totals_ = [None if first else rest[0][head] for head in range(NH)]
    for block, (a_ref, k_ref, p_ref) in enumerate(((a0, k0, p0), (a1, k1, p1))):
        row = rows_of(block)
        dens = jnp.zeros((BLOCK, DH), BF)
        for head in range(NH):
            col = cols(head)
            fq = f_ref[row, col]
            grad = k_ref[:, col] + p_ref[:, col].astype(F32)
            inv = r_ref[row, col]
            num = (grad * inv).astype(BF)
            gn_ref[row, col] = num
            den = -jnp.sum(grad * a_ref[:, col].astype(F32), axis=1, keepdims=True) * inv
            upper = den.astype(BF)
            lower = (den - upper.astype(F32)).astype(BF)
            dens = jnp.where(lane == 2 * head, upper, dens)
            dens = jnp.where(lane == 2 * head + 1, lower, dens)
            sums = with_row(
                dot(num, fq, TN), jnp.sum(den * fq.astype(F32), axis=0, keepdims=True)
            )
            sum_ref[block, head] = sums
            before = totals_[head]
            totals_[head] = sums if before is None else before + sums
        den_ref[row] = dens
    if first:
        for head in range(NH):
            tot_ref[head] = totals_[head]
    else:
        split(place()[1], totals_, tot_ref, rest[5])


def numden(f, r, a, keep, got, before, after):
    return call(
        numden_kernel,
        "numden",
        (f, r, *a, *keep, *got, *before),
        [
            ((2 * BLOCK, NH * DH), BF),
            ((2 * BLOCK, DH), BF),
            ((2, NH, ROWS, DH), F32),
            *([(HALF_STATE, F32)] * 2 if before else [((NH, ROWS, DH), F32)]),
        ],
        after,
    )


def local_kernel(
    block, f_ref, k_ref, v_ref, n_ref, d_ref, loc_ref, mine, back, *rest
):
    gq_ref, gk_ref, gv_ref = rest[-3:]
    _, core, _, _ = place()
    causal = lax.broadcasted_iota(jnp.int32, (HALF, HALF), 0) <= lax.broadcasted_iota(
        jnp.int32, (HALF, HALF), 1
    )
    lane = lax.broadcasted_iota(jnp.int32, (BLOCK, DH), 1)
    top, low = slice(0, HALF), slice(HALF, BLOCK)
    near, row = rows_of(block % 2), rows_of(block)
    dens = d_ref[near]
    for head in range(NH):
        col = cols(head)
        fq = f_ref[near, col]
        fk = k_ref[row, col]
        num = n_ref[near, col]
        pick = ((lane == 2 * head) | (lane == 2 * head + 1)).astype(F32).astype(BF)
        left = jnp.concatenate([v_ref[row, col], pick], axis=1)
        right = jnp.concatenate([num, dens], axis=1)

        def pair(a, b, s, t, mask):
            out = dot(a[s], b[t], NT)
            return (jnp.where(causal, out, 0.0) if mask else out).astype(BF)

        w00 = pair(fk, fq, top, top, True)
        w01 = pair(fk, fq, top, low, False)
        w11 = pair(fk, fq, low, low, True)
        g00 = pair(left, right, top, top, True)
        g01 = pair(left, right, top, low, False)
        g11 = pair(left, right, low, low, True)
        gv_ref[top, col] = dot(jnp.concatenate([w00, w01], axis=1), num, NN)
        gv_ref[low, col] = dot(w11, num[low], NN)
        gk_ref[top, col] = dot(jnp.concatenate([g00, g01], axis=1), fq, NN)
        gk_ref[low, col] = dot(g11, fq[low], NN)
        state = whole(core, (mine, back), head) + loc_ref[block, head]
        past = dot(
            jnp.concatenate([num, num], axis=1),
            jnp.concatenate(halves(state[:DH]), axis=0),
            NN,
        )
        den = dens[:, 2 * head : 2 * head + 1].astype(F32) + dens[
            :, 2 * head + 1 : 2 * head + 2
        ].astype(F32)
        past = past + den * state[DH : DH + 1]
        tilt = jnp.minimum(fq.astype(F32), 1.0)
        gq_ref[row.start : row.start + HALF, col] = (tilt[top] * (past[top] + dot(g00, fk[top], TN))).astype(BF)
        gq_ref[row.start + HALF : row.stop, col] = (
            tilt[low]
            * (past[low] + dot(jnp.concatenate([g01, g11], axis=0), fk, TN))
        ).astype(BF)


def local(f, fk, v, num, den, loc, prior, block, before, after):
    shape = (BLOCK, NH * DH)
    return call(
        functools.partial(local_kernel, block),
        "local",
        (f, fk, v, num, den, loc, *prior, *before),
        [((NB * BLOCK, NH * DH), BF), (shape, F32), (shape, F32)],
        after,
        aliases={8: 0} if before else None,
    )


def later_kernel(k_ref, v_ref, gq_ref, ka, kb, ga, gb, *rest):
    near, (s0_ref, s1_ref, mine, back) = rest[:8], rest[8:12]
    out_hbm, gq_hbm, gk_hbm, gv_hbm, out_ref, gk_ref, gv_ref, sems = rest[12:]
    _, core, _, _ = place()
    copies = []

    def send(source, target):
        copies.append(pltpu.make_async_copy(source, target, sems.at[len(copies)]))
        copies[-1].start()

    send(gq_ref, gq_hbm)
    for block, (keep, got) in enumerate(((ka, ga), (kb, gb))):
        row = rows_of(block)
        out_ref[row] = (keep[...] + got[...].astype(F32)).astype(BF)
        send(out_ref.at[row], out_hbm.at[row])
    states = [whole(core, (mine, back), head) for head in range(NH)]
    for block in reversed(range(NB)):
        row = rows_of(block)
        for head in range(NH):
            col = cols(head)
            fk = k_ref[row, col]
            val = v_ref[row, col]
            upper, lower = halves(states[head][:DH])
            gk = near[2 * block][:, col] + dot(
                jnp.concatenate([val, val], axis=1),
                jnp.concatenate([upper, lower], axis=0),
                NN,
            )
            gk = gk + states[head][DH : DH + 1]
            gk_ref[row, col] = (jnp.minimum(fk.astype(F32), 1.0) * gk).astype(BF)
            gv = near[2 * block + 1][:, col] + dot(
                jnp.concatenate([fk, fk], axis=1),
                jnp.concatenate([upper, lower], axis=1),
                NT,
            )
            gv_ref[row, col] = gv.astype(BF)
            if block:
                states[head] = states[head] + (s0_ref, s1_ref)[block // 2][block % 2, head]
        send(gk_ref.at[row], gk_hbm.at[row])
        send(gv_ref.at[row], gv_hbm.at[row])
    for copy in copies:
        copy.wait()


def later(fk, v, gq, keep, got, near, s0, s1, behind):
    full = (NB * BLOCK, NH * DH)
    args = (fk, v, gq, *keep, *got, *near, s0, s1, *behind)
    return pl.pallas_call(
        later_kernel,
        in_specs=[VMEM] * len(args),
        out_specs=[HBM] * 4,
        out_shape=[jax.ShapeDtypeStruct(full, BF)] * 4,
        scratch_shapes=[
            pltpu.VMEM((2 * BLOCK, NH * DH), BF),
            pltpu.VMEM(full, BF),
            pltpu.VMEM(full, BF),
            pltpu.SemaphoreType.DMA((3 + 2 * NB,)),
        ],
        compiler_params=PARAMS,
        name="later",
    )(*args)


A_PAIRS = [(h, h ^ 1) for h in range(4)]
B_PAIRS = [(h, 3 - h) for h in range(4)]


def ctx_pairs(change):
    out = []
    for y in range(4):
        for z in range(4):
            for c in range(2):
                y2, z2, c2 = change(y, z, c)
                out.append((y * 8 + z * 2 + c, y2 * 8 + z2 * 2 + c2))
    return out


def swap(x, change):
    return lax.ppermute(x, "ctx", ctx_pairs(change))


def sibling(x):
    return swap(x, lambda y, z, c: (y, z, 1 - c))


def flags(reverse):
    _, core, z, y = place()
    if reverse:
        return core == 0, z % 2 == 0, z < 2, y % 2 == 0, y < 2
    return core == 1, z % 2 == 1, z >= 2, y % 2 == 1, y >= 2


def add_kernel(a_ref, b_ref, out_ref):
    out_ref[...] = a_ref[...] + b_ref[...]


def column_kernel(reverse, chip, near, far, both):
    _, _, _, odd, high = flags(reverse)
    both[0] = jnp.where(odd, near[...], 0.0) + jnp.where(high, far[...], 0.0)
    both[1] = chip[...]


def row_kernel(reverse, own, got, message, partial):
    _, odd, high, _, _ = flags(reverse)
    column = own[0] + got[0]
    message[...] = column + jnp.where(high, 0.0, own[1] + got[1])
    partial[...] = column + jnp.where(odd, got[1], 0.0)


def last_kernel(reverse, partial, more, mine, got, my, its):
    second, _, _, _, _ = flags(reverse)
    ahead = partial[...] + more[...]
    my[...] = ahead + jnp.where(second, got[...], 0.0)
    its[...] = ahead + jnp.where(second, 0.0, mine[...])


def entering(mine, other, reverse):
    one = [(HALF_STATE, F32)]
    got, after = yield other, lambda y, z, c: (y, z, 1 - c)
    (chip,) = call(add_kernel, "chip", (mine, got), one, after)
    near, after = yield chip, lambda y, z, c: (y ^ 1, z, c)
    (pair,) = call(add_kernel, "pair", (chip, near), one, after)
    far, after = yield pair, lambda y, z, c: (3 - y, z, c)
    (both,) = call(
        functools.partial(column_kernel, reverse),
        "column",
        (chip, near, far),
        [((2, *HALF_STATE), F32)],
        after,
    )
    swapped, after = yield both, lambda y, z, c: (y, z ^ 1, c)
    message, partial = call(
        functools.partial(row_kernel, reverse), "row", (both, swapped), one * 2, after
    )
    more, after = yield message, lambda y, z, c: (y, 3 - z, c)
    my, its = call(
        functools.partial(last_kernel, reverse),
        "last",
        (partial, more, mine, got),
        one * 2,
        after,
    )
    back, after = yield its, lambda y, z, c: (y, z, 1 - c)
    yield (my, back), None


class Scan:
    def __init__(self, mine, other, reverse):
        self.steps = entering(mine, other, reverse)
        self.moved = None

    def _next(self, after):
        return next(self.steps) if self.moved is None else self.steps.send((self.moved, after))

    def hop(self, *after):
        message, move = self._next(after)
        self.moved = swap(message, move)
        return message

    def result(self):
        return self._next(())[0]


def on_device(queries, key_input, value_input, out_weight, cotangent):
    def to_x(x):
        return lax.ppermute(x, "head", A_PAIRS)

    def to_d(x):
        return lax.ppermute(x, "head", B_PAIRS)

    piece = ((BLOCK, NH * DH), BF)
    part = ((HALF, NH * DH), BF)
    a_send, b_send, block0, block1 = stage(
        first_pieces, "first", (out_weight, cotangent), [part, part, piece, piece]
    )
    block2, block3, *own = stage(
        second_pieces, "second", (out_weight, cotangent), [piece] * 5, (a_send,)
    )
    blocks = (block0, block1, block2, block3)
    a_own, b_own = to_x(a_send), to_d(b_send)

    loc, fk, mine, other = totals(key_input, value_input, (block2,))
    cots = [(to_x(tie(block0, mine, a_own)), to_d(tie(block1, mine, b_own)))]
    cots.append((to_x(tie(block2, cots[0][0])), to_d(tie(block3, cots[0][1]))))
    scan = Scan(mine, other, False)
    scan.hop()
    sent = scan.hop()
    a_got = swap(a_own, lambda y, z, c: (y ^ 1, z, c))
    b_got = swap(b_own, lambda y, z, c: (y, z ^ 1, c))
    near0 = inside(queries, fk, value_input, 0, (sent, a_own, b_own))
    (quarters,) = call(
        assemble_kernel,
        "assemble",
        (a_own, a_got, b_own, b_got),
        [((2, BLOCK, NH * DH), BF)],
        (near0[0], *cots[0]),
    )
    weights = (*own, quarters, sibling(quarters))
    sent = scan.hop(near0[0])
    near = [near0, None]
    sent = scan.hop(quarters)

    def grad_project(c, after):
        keep_a, keep_b, send_x, send_d = project(
            NT, blocks[2 * c], blocks[2 * c + 1], *cots[c], weights, after
        )
        return (keep_a, keep_b), (to_d(send_d), to_x(send_x))

    grads = [grad_project(0, (sent,)), None]
    sent = scan.hop(grads[0][0][0])
    grads[1] = grad_project(1, (sent,))
    sent = scan.hop(grads[1][0][0])
    near[1] = inside(queries, fk, value_input, 1, (sent,))
    prior = scan.result()
    heads = [attend(near[0], loc, prior, 0, (near[1][0],))]
    heads.append(attend(near[1], loc, prior, 1, (heads[0][0],)))
    gathered = [(to_x(heads[c][0]), to_d(heads[c][1])) for c in range(2)]

    nums = []
    for c in range(2):
        before = (nums[0][3],) if c else ()
        nums.append(numden(near[c][0], heads[c][2], heads[c][:2], *grads[c], before, ()))
    scan = Scan(*nums[1][3:], True)

    def out_project(c, after):
        keep_a, keep_b, send_x, send_d = project(
            NN, *heads[c][:2], *gathered[c], weights, after
        )
        return (keep_a, keep_b), (to_d(send_d), to_x(send_x))

    parts = []

    def local_block(block, after):
        c = block // 2
        before = (parts[-1][0],) if parts else ()
        parts.append(
            local(
                near[c][0],
                fk,
                value_input,
                *nums[c][:2],
                loc,
                prior,
                block,
                before,
                after,
            )
        )
        return parts[-1][1]

    sent = scan.hop()
    done = local_block(0, (sent,))
    sent = scan.hop(done)
    done = local_block(1, (sent,))
    sent = scan.hop(done)
    out0 = out_project(0, (sent,))
    sent = scan.hop(out0[0][0])
    done = local_block(2, (sent, out0[0][0]))
    sent = scan.hop(done)
    out1 = out_project(1, (sent,))
    done = local_block(3, (out1[0][0],))
    scan.hop(done)
    out, grad_query, grad_key, grad_value = later(
        fk,
        value_input,
        parts[-1][0],
        *out0,
        [x for part in parts for x in part[1:]],
        nums[0][2],
        nums[1][2],
        scan.result(),
    )
    return finish(*out1, out), grad_query, grad_key, grad_value


def solution(mesh):
    in_specs = (
        P("ctx", "head"),
        P("ctx", "head"),
        P("ctx", "head"),
        P("head", None),
        P("ctx", "head"),
    )
    out_specs = (P("ctx", "head"), P("ctx", "head"), P("ctx", "head"), P("ctx", "head"))
    return jax.shard_map(
        on_device, mesh=mesh, in_specs=in_specs, out_specs=out_specs, check_vma=False
    )
```

```python
import functools

import jax
import jax.numpy as jnp
from jax import lax
from jax.experimental import pallas as pl
from jax.experimental.pallas import tpu as pltpu
from jax.sharding import PartitionSpec as P

DH = 128
BLOCK = 512
HALF = BLOCK // 2
NH = 4
NB = 4
ROWS = DH + 8
BF = jnp.bfloat16
F32 = jnp.float32

PARAMS = pltpu.CompilerParams(vmem_limit_bytes=14 * 1024 * 1024)
VMEM = pl.BlockSpec(memory_space=pltpu.VMEM)
HBM = pl.BlockSpec(memory_space=pltpu.HBM)

NN = (((1,), (0,)), ((), ()))
NT = (((1,), (1,)), ((), ()))
TN = (((0,), (0,)), ((), ()))


def dot(a, b, dims):
    return lax.dot_general(a, b, dims, preferred_element_type=F32)


def feature(lifted):
    return jnp.where(lifted > 0, lifted + 1.0, jnp.exp(jnp.minimum(lifted, 0.0)))


def slope(lifted):
    return jnp.where(lifted > 0, 1.0, jnp.exp(jnp.minimum(lifted, 0.0)))


def halves(state):
    upper = state.astype(BF)
    return upper, (state - upper.astype(F32)).astype(BF)


def call(kernel, name, args, outs, after=(), aliases=None):
    count, extra = len(args), len(after)

    def body(*refs):
        kernel(*refs[:count], *refs[count + extra :])

    return pl.pallas_call(
        body,
        in_specs=[VMEM] * (count + extra),
        out_specs=[VMEM] * len(outs),
        out_shape=[pltpu.VMEM(shape, dtype) for shape, dtype in outs],
        input_output_aliases=aliases or {},
        compiler_params=PARAMS,
        name=name,
    )(*args, *after)


def place():
    head, index = lax.axis_index("head"), lax.axis_index("ctx")
    return head, index % 2, (index // 2) % 4, index // 8


def partner(head):
    return head + 1 - 2 * (head % 2)


def tie(x, *after):
    return lax.optimization_barrier((x, *after))[0] if after else x


def cols(head):
    return slice(head * DH, (head + 1) * DH)


def rows_of(block):
    return slice(block * BLOCK, (block + 1) * BLOCK)


def with_row(state, row):
    return jnp.concatenate([state, jnp.broadcast_to(row, (ROWS - DH, DH))], axis=0)


def stage(kernel, name, args, outs, after=()):
    args = tuple(pltpu.with_memory_space_constraint(x, pltpu.HBM) for x in args)
    count, extra = len(args), len(after)

    def body(*refs):
        sems = refs[-1]
        copies = [
            pltpu.make_async_copy(source, target, sems.at[i])
            for i, (source, target) in enumerate(
                zip(kernel(*refs[:count]), refs[count + extra : -1])
            )
        ]
        for copy in copies:
            copy.start()
        for copy in copies:
            copy.wait()

    return pl.pallas_call(
        body,
        in_specs=[HBM] * count + [VMEM] * extra,
        out_specs=[VMEM] * len(outs),
        out_shape=[pltpu.VMEM(shape, dtype) for shape, dtype in outs],
        scratch_shapes=[pltpu.SemaphoreType.DMA((len(outs),))],
        compiler_params=PARAMS,
        name=name,
    )(*args, *after)


def quarter(w_ref, index, rows=slice(None)):
    size = NH * DH
    return w_ref.at[rows, pl.ds(pl.multiple_of(index * size, size), size)]


def half_rows(which):
    return pl.ds(pl.multiple_of(which * HALF, HALF), HALF)


def first_pieces(w_ref, c_ref):
    head, core, z, y = place()
    x, d = partner(head), 3 - head
    return (
        quarter(w_ref, x + core * (3 - 2 * x), half_rows(y % 2)),
        quarter(w_ref, d + core * (partner(d) - d), half_rows(z % 2)),
        c_ref.at[rows_of(0)],
        c_ref.at[rows_of(1)],
    )


def second_pieces(w_ref, c_ref):
    head, _, _, _ = place()
    return (
        c_ref.at[rows_of(2)],
        c_ref.at[rows_of(3)],
        quarter(w_ref, head),
        quarter(w_ref, partner(head)),
        quarter(w_ref, 3 - head),
    )


def assemble_kernel(a_own, a_got, b_own, b_got, out_ref):
    _, _, z, y = place()
    out_ref[0, half_rows(y % 2)] = a_own[...]
    out_ref[0, half_rows(1 - y % 2)] = a_got[...]
    out_ref[1, half_rows(z % 2)] = b_own[...]
    out_ref[1, half_rows(1 - z % 2)] = b_got[...]


HALF_STATE = (NH // 2, ROWS, DH)


def split(core, sums, mine_ref, other_ref):
    for i in range(NH // 2):
        low, high = sums[i], sums[NH // 2 + i]
        mine_ref[i] = jnp.where(core == 0, low, high)
        other_ref[i] = jnp.where(core == 0, high, low)


def whole(core, pair, head):
    mine, back = pair
    slot = head % (NH // 2)
    return jnp.where(core == head // (NH // 2), mine[slot], back[slot])


def totals_kernel(k_ref, v_ref, loc_ref, fk_ref, mine_ref, other_ref):
    _, core, _, _ = place()
    sums = []
    for head in range(NH):
        col = cols(head)
        total = jnp.zeros((ROWS, DH), F32)
        for block in range(NB):
            row = rows_of(block)
            feat = feature(k_ref[row, col].astype(F32)).astype(BF)
            fk_ref[row, col] = feat
            loc_ref[block, head] = total
            total = total + with_row(
                dot(v_ref[row, col], feat, TN),
                jnp.sum(feat.astype(F32), axis=0, keepdims=True),
            )
        sums.append(total)
    split(core, sums, mine_ref, other_ref)


def totals(k, v, after):
    return call(
        totals_kernel,
        "totals",
        (k, v),
        [((NB, NH, ROWS, DH), F32), ((NB * BLOCK, NH * DH), BF), (HALF_STATE, F32), (HALF_STATE, F32)],
        after,
    )


def inside_kernel(chunk, q_ref, k_ref, v_ref, f_ref, n_ref, d_ref):
    lower = lax.broadcasted_iota(jnp.int32, (HALF, HALF), 0) >= lax.broadcasted_iota(
        jnp.int32, (HALF, HALF), 1
    )
    ones = jnp.ones((BLOCK, DH), BF)
    for block in range(2):
        row = rows_of(2 * chunk + block)
        base = block * BLOCK
        for head in range(NH):
            col = cols(head)
            fq = feature(q_ref[row, col].astype(F32)).astype(BF)
            f_ref[base : base + BLOCK, col] = fq
            fk = k_ref[row, col]
            wide = jnp.concatenate([v_ref[row, col], ones], axis=1)
            w00 = jnp.where(lower, dot(fq[:HALF], fk[:HALF], NT), 0.0).astype(BF)
            w10 = dot(fq[HALF:], fk[:HALF], NT).astype(BF)
            w11 = jnp.where(lower, dot(fq[HALF:], fk[HALF:], NT), 0.0).astype(BF)
            top = dot(w00, wide[:HALF], NN)
            low = dot(jnp.concatenate([w10, w11], axis=1), wide, NN)
            n_ref[base : base + HALF, col] = top[:, :DH]
            d_ref[base : base + HALF, col] = top[:, DH:]
            n_ref[base + HALF : base + BLOCK, col] = low[:, :DH]
            d_ref[base + HALF : base + BLOCK, col] = low[:, DH:]


def inside(q, fk, v, chunk, after):
    shape = (2 * BLOCK, NH * DH)
    return call(
        functools.partial(inside_kernel, chunk),
        "inside",
        (q, fk, v),
        [(shape, BF), (shape, F32), (shape, F32)],
        after,
    )


def attend_kernel(chunk, f_ref, n_ref, d_ref, loc_ref, mine, back, a0, a1, r_ref):
    _, core, _, _ = place()
    for block, a_ref in enumerate((a0, a1)):
        row = rows_of(block)
        for head in range(NH):
            col = cols(head)
            fq = f_ref[row, col]
            state = whole(core, (mine, back), head) + loc_ref[2 * chunk + block, head]
            both = jnp.concatenate(
                [state[:DH], jnp.broadcast_to(state[DH : DH + 1], (DH, DH))], axis=0
            )
            sums = jnp.concatenate(halves(both), axis=1)
            past = dot(jnp.concatenate([fq, fq], axis=1), sums, NT)
            inv = 1.0 / (past[:, DH:] + d_ref[row, col])
            r_ref[row, col] = inv
            a_ref[:, col] = ((past[:, :DH] + n_ref[row, col]) * inv).astype(BF)


def attend(near, loc, prior, chunk, after):
    return call(
        functools.partial(attend_kernel, chunk),
        "attend",
        (*near, loc, *prior),
        [((BLOCK, NH * DH), BF)] * 2 + [((2 * BLOCK, NH * DH), F32)],
        after,
    )


def project_kernel(
    dims, xa, xb, ga, gb, wh, wx, wd, mine, other, keep_a, keep_b, to_x, to_d
):
    _, core, _, _ = place()
    even = core == 0
    a_h = jnp.where(even, mine[0], other[0])
    a_d = jnp.where(even, other[0], mine[0])
    b_h = jnp.where(even, mine[1], other[1])
    b_x = jnp.where(even, other[1], mine[1])
    if dims == NT:
        ka, sa, kb, sb = wx[...], (b_h, b_x), wd[...], (a_h, a_d)
    else:
        ka, sa, kb, sb = a_h, (wd[...], a_d), b_h, (wx[...], b_x)
    to_d[...] = (dot(xa[...], sa[0], dims) + dot(ga[...], sa[1], dims)).astype(BF)
    to_x[...] = (dot(xb[...], sb[0], dims) + dot(gb[...], sb[1], dims)).astype(BF)
    keep_a[...] = dot(xa[...], wh[...], dims) + dot(ga[...], ka, dims)
    keep_b[...] = dot(xb[...], wh[...], dims) + dot(gb[...], kb, dims)


def project(dims, xa, xb, ga, gb, weights, after):
    shape = (BLOCK, NH * DH)
    return call(
        functools.partial(project_kernel, dims),
        "project",
        (xa, xb, ga, gb, *weights),
        [(shape, F32)] * 2 + [(shape, BF)] * 2,
        after,
    )


def finish_kernel(ka, kb, ga, gb, whole_ref, out_ref, rows_ref, sem):
    del whole_ref
    copies = []
    for block, (keep, got) in enumerate(((ka, ga), (kb, gb))):
        row = rows_of(block)
        rows_ref[row] = (keep[...] + got[...].astype(F32)).astype(BF)
        copies.append(
            pltpu.make_async_copy(
                rows_ref.at[row], out_ref.at[rows_of(2 + block)], sem.at[block]
            )
        )
        copies[-1].start()
    for copy in copies:
        copy.wait()


def finish(keep, got, whole_out):
    return pl.pallas_call(
        finish_kernel,
        in_specs=[VMEM] * 4 + [HBM],
        out_specs=HBM,
        out_shape=jax.ShapeDtypeStruct((NB * BLOCK, NH * DH), BF),
        scratch_shapes=[
            pltpu.VMEM((2 * BLOCK, NH * DH), BF),
            pltpu.SemaphoreType.DMA((2,)),
        ],
        input_output_aliases={4: 0},
        compiler_params=PARAMS,
        name="finish",
    )(*keep, *got, whole_out)


def numden_kernel(f_ref, r_ref, a0, a1, k0, k1, p0, p1, *rest):
    first = len(rest) == 4
    gn_ref, den_ref, sum_ref, tot_ref = rest if first else rest[1:5]
    lane = lax.broadcasted_iota(jnp.int32, (BLOCK, DH), 1)
    totals_ = [None if first else rest[0][head] for head in range(NH)]
    for block, (a_ref, k_ref, p_ref) in enumerate(((a0, k0, p0), (a1, k1, p1))):
        row = rows_of(block)
        dens = jnp.zeros((BLOCK, DH), BF)
        for head in range(NH):
            col = cols(head)
            fq = f_ref[row, col]
            grad = k_ref[:, col] + p_ref[:, col].astype(F32)
            inv = r_ref[row, col]
            num = (grad * inv).astype(BF)
            gn_ref[row, col] = num
            den = -jnp.sum(grad * a_ref[:, col].astype(F32), axis=1, keepdims=True) * inv
            upper = den.astype(BF)
            lower = (den - upper.astype(F32)).astype(BF)
            dens = jnp.where(lane == 2 * head, upper, dens)
            dens = jnp.where(lane == 2 * head + 1, lower, dens)
            sums = with_row(
                dot(num, fq, TN), jnp.sum(den * fq.astype(F32), axis=0, keepdims=True)
            )
            sum_ref[block, head] = sums
            before = totals_[head]
            totals_[head] = sums if before is None else before + sums
        den_ref[row] = dens
    if first:
        for head in range(NH):
            tot_ref[head] = totals_[head]
    else:
        split(place()[1], totals_, tot_ref, rest[5])


def numden(f, r, a, keep, got, before, after):
    return call(
        numden_kernel,
        "numden",
        (f, r, *a, *keep, *got, *before),
        [
            ((2 * BLOCK, NH * DH), BF),
            ((2 * BLOCK, DH), BF),
            ((2, NH, ROWS, DH), F32),
            *([(HALF_STATE, F32)] * 2 if before else [((NH, ROWS, DH), F32)]),
        ],
        after,
    )


def local_kernel(
    block, f_ref, k_ref, v_ref, n_ref, d_ref, loc_ref, mine, back, *rest
):
    gq_ref, gk_ref, gv_ref = rest[-3:]
    _, core, _, _ = place()
    causal = lax.broadcasted_iota(jnp.int32, (HALF, HALF), 0) <= lax.broadcasted_iota(
        jnp.int32, (HALF, HALF), 1
    )
    lane = lax.broadcasted_iota(jnp.int32, (BLOCK, DH), 1)
    top, low = slice(0, HALF), slice(HALF, BLOCK)
    near, row = rows_of(block % 2), rows_of(block)
    dens = d_ref[near]
    for head in range(NH):
        col = cols(head)
        fq = f_ref[near, col]
        fk = k_ref[row, col]
        num = n_ref[near, col]
        pick = ((lane == 2 * head) | (lane == 2 * head + 1)).astype(F32).astype(BF)
        left = jnp.concatenate([v_ref[row, col], pick], axis=1)
        right = jnp.concatenate([num, dens], axis=1)

        def pair(a, b, s, t, mask):
            out = dot(a[s], b[t], NT)
            return (jnp.where(causal, out, 0.0) if mask else out).astype(BF)

        w00 = pair(fk, fq, top, top, True)
        w01 = pair(fk, fq, top, low, False)
        w11 = pair(fk, fq, low, low, True)
        g00 = pair(left, right, top, top, True)
        g01 = pair(left, right, top, low, False)
        g11 = pair(left, right, low, low, True)
        gv_ref[top, col] = dot(jnp.concatenate([w00, w01], axis=1), num, NN)
        gv_ref[low, col] = dot(w11, num[low], NN)
        gk_ref[top, col] = dot(jnp.concatenate([g00, g01], axis=1), fq, NN)
        gk_ref[low, col] = dot(g11, fq[low], NN)
        state = whole(core, (mine, back), head) + loc_ref[block, head]
        past = dot(
            jnp.concatenate([num, num], axis=1),
            jnp.concatenate(halves(state[:DH]), axis=0),
            NN,
        )
        den = dens[:, 2 * head : 2 * head + 1].astype(F32) + dens[
            :, 2 * head + 1 : 2 * head + 2
        ].astype(F32)
        past = past + den * state[DH : DH + 1]
        tilt = jnp.minimum(fq.astype(F32), 1.0)
        gq_ref[row.start : row.start + HALF, col] = (tilt[top] * (past[top] + dot(g00, fk[top], TN))).astype(BF)
        gq_ref[row.start + HALF : row.stop, col] = (
            tilt[low]
            * (past[low] + dot(jnp.concatenate([g01, g11], axis=0), fk, TN))
        ).astype(BF)


def local(f, fk, v, num, den, loc, prior, block, before, after):
    shape = (BLOCK, NH * DH)
    return call(
        functools.partial(local_kernel, block),
        "local",
        (f, fk, v, num, den, loc, *prior, *before),
        [((NB * BLOCK, NH * DH), BF), (shape, F32), (shape, F32)],
        after,
        aliases={8: 0} if before else None,
    )


def later_kernel(k_ref, v_ref, gq_ref, ka, kb, ga, gb, *rest):
    near, (s0_ref, s1_ref, mine, back) = rest[:8], rest[8:12]
    out_hbm, gq_hbm, gk_hbm, gv_hbm, out_ref, gk_ref, gv_ref, sems = rest[12:]
    _, core, _, _ = place()
    copies = []

    def send(source, target):
        copies.append(pltpu.make_async_copy(source, target, sems.at[len(copies)]))
        copies[-1].start()

    send(gq_ref, gq_hbm)
    for block, (keep, got) in enumerate(((ka, ga), (kb, gb))):
        row = rows_of(block)
        out_ref[row] = (keep[...] + got[...].astype(F32)).astype(BF)
        send(out_ref.at[row], out_hbm.at[row])
    states = [whole(core, (mine, back), head) for head in range(NH)]
    for block in reversed(range(NB)):
        row = rows_of(block)
        for head in range(NH):
            col = cols(head)
            fk = k_ref[row, col]
            val = v_ref[row, col]
            upper, lower = halves(states[head][:DH])
            gk = near[2 * block][:, col] + dot(
                jnp.concatenate([val, val], axis=1),
                jnp.concatenate([upper, lower], axis=0),
                NN,
            )
            gk = gk + states[head][DH : DH + 1]
            gk_ref[row, col] = (jnp.minimum(fk.astype(F32), 1.0) * gk).astype(BF)
            gv = near[2 * block + 1][:, col] + dot(
                jnp.concatenate([fk, fk], axis=1),
                jnp.concatenate([upper, lower], axis=1),
                NT,
            )
            gv_ref[row, col] = gv.astype(BF)
            if block:
                states[head] = states[head] + (s0_ref, s1_ref)[block // 2][block % 2, head]
        send(gk_ref.at[row], gk_hbm.at[row])
        send(gv_ref.at[row], gv_hbm.at[row])
    for copy in copies:
        copy.wait()


def later(fk, v, gq, keep, got, near, s0, s1, behind):
    full = (NB * BLOCK, NH * DH)
    args = (fk, v, gq, *keep, *got, *near, s0, s1, *behind)
    return pl.pallas_call(
        later_kernel,
        in_specs=[VMEM] * len(args),
        out_specs=[HBM] * 4,
        out_shape=[jax.ShapeDtypeStruct(full, BF)] * 4,
        scratch_shapes=[
            pltpu.VMEM((2 * BLOCK, NH * DH), BF),
            pltpu.VMEM(full, BF),
            pltpu.VMEM(full, BF),
            pltpu.SemaphoreType.DMA((3 + 2 * NB,)),
        ],
        compiler_params=PARAMS,
        name="later",
    )(*args)


A_PAIRS = [(h, h ^ 1) for h in range(4)]
B_PAIRS = [(h, 3 - h) for h in range(4)]


def ctx_pairs(change):
    out = []
    for y in range(4):
        for z in range(4):
            for c in range(2):
                y2, z2, c2 = change(y, z, c)
                out.append((y * 8 + z * 2 + c, y2 * 8 + z2 * 2 + c2))
    return out


def swap(x, change):
    return lax.ppermute(x, "ctx", ctx_pairs(change))


def sibling(x):
    return swap(x, lambda y, z, c: (y, z, 1 - c))


def flags(reverse):
    _, core, z, y = place()
    if reverse:
        return core == 0, z % 2 == 0, z < 2, y % 2 == 0, y < 2
    return core == 1, z % 2 == 1, z >= 2, y % 2 == 1, y >= 2


def add_kernel(a_ref, b_ref, out_ref):
    out_ref[...] = a_ref[...] + b_ref[...]


def column_kernel(reverse, chip, near, far, both):
    _, _, _, odd, high = flags(reverse)
    both[0] = jnp.where(odd, near[...], 0.0) + jnp.where(high, far[...], 0.0)
    both[1] = chip[...]


def row_kernel(reverse, own, got, message, partial):
    _, odd, high, _, _ = flags(reverse)
    column = own[0] + got[0]
    message[...] = column + jnp.where(high, 0.0, own[1] + got[1])
    partial[...] = column + jnp.where(odd, got[1], 0.0)


def last_kernel(reverse, partial, more, mine, got, my, its):
    second, _, _, _, _ = flags(reverse)
    ahead = partial[...] + more[...]
    my[...] = ahead + jnp.where(second, got[...], 0.0)
    its[...] = ahead + jnp.where(second, 0.0, mine[...])


def entering(mine, other, reverse):
    one = [(HALF_STATE, F32)]
    got, after = yield other, lambda y, z, c: (y, z, 1 - c)
    (chip,) = call(add_kernel, "chip", (mine, got), one, after)
    near, after = yield chip, lambda y, z, c: (y ^ 1, z, c)
    (pair,) = call(add_kernel, "pair", (chip, near), one, after)
    far, after = yield pair, lambda y, z, c: (3 - y, z, c)
    (both,) = call(
        functools.partial(column_kernel, reverse),
        "column",
        (chip, near, far),
        [((2, *HALF_STATE), F32)],
        after,
    )
    swapped, after = yield both, lambda y, z, c: (y, z ^ 1, c)
    message, partial = call(
        functools.partial(row_kernel, reverse), "row", (both, swapped), one * 2, after
    )
    more, after = yield message, lambda y, z, c: (y, 3 - z, c)
    my, its = call(
        functools.partial(last_kernel, reverse),
        "last",
        (partial, more, mine, got),
        one * 2,
        after,
    )
    back, after = yield its, lambda y, z, c: (y, z, 1 - c)
    yield (my, back), None


class Scan:
    def __init__(self, mine, other, reverse):
        self.steps = entering(mine, other, reverse)
        self.moved = None

    def _next(self, after):
        return next(self.steps) if self.moved is None else self.steps.send((self.moved, after))

    def hop(self, *after):
        message, move = self._next(after)
        self.moved = swap(message, move)
        return message

    def result(self):
        return self._next(())[0]


def on_device(queries, key_input, value_input, out_weight, cotangent):
    def to_x(x):
        return lax.ppermute(x, "head", A_PAIRS)

    def to_d(x):
        return lax.ppermute(x, "head", B_PAIRS)

    piece = ((BLOCK, NH * DH), BF)
    part = ((HALF, NH * DH), BF)
    a_send, b_send, block0, block1 = stage(
        first_pieces, "first", (out_weight, cotangent), [part, part, piece, piece]
    )
    block2, block3, *own = stage(
        second_pieces, "second", (out_weight, cotangent), [piece] * 5, (a_send,)
    )
    blocks = (block0, block1, block2, block3)
    a_own, b_own = to_x(a_send), to_d(b_send)

    loc, fk, mine, other = totals(key_input, value_input, (block2,))
    cots = [(to_x(tie(block0, mine, a_own)), to_d(tie(block1, mine, b_own)))]
    cots.append((to_x(tie(block2, cots[0][0])), to_d(tie(block3, cots[0][1]))))
    scan = Scan(mine, other, False)
    scan.hop()
    sent = scan.hop()
    a_got = swap(a_own, lambda y, z, c: (y ^ 1, z, c))
    b_got = swap(b_own, lambda y, z, c: (y, z ^ 1, c))
    near = [inside(queries, fk, value_input, 0, (sent, a_own, b_own))]
    sent = scan.hop(near[0][0])
    (quarters,) = call(
        assemble_kernel,
        "assemble",
        (a_own, a_got, b_own, b_got),
        [((2, BLOCK, NH * DH), BF)],
        (near[0][0], sent, *cots[0]),
    )
    weights = (*own, quarters, sibling(quarters))

    def grad_project(c, after):
        keep_a, keep_b, send_x, send_d = project(
            NT, blocks[2 * c], blocks[2 * c + 1], *cots[c], weights, after
        )
        return (keep_a, keep_b), (to_d(send_d), to_x(send_x))

    grads = [grad_project(0, (sent,))]
    sent = scan.hop(grads[0][0][0])
    near.append(inside(queries, fk, value_input, 1, (sent,)))
    sent = scan.hop(near[1][0])
    grads.append(grad_project(1, (sent,)))
    scan.hop(grads[1][0][0])
    prior = scan.result()
    heads = [attend(near[0], loc, prior, 0, (near[1][0],))]
    heads.append(attend(near[1], loc, prior, 1, (heads[0][0],)))
    gathered = [(to_x(heads[c][0]), to_d(heads[c][1])) for c in range(2)]

    nums = []
    for c in range(2):
        before = (nums[0][3],) if c else ()
        nums.append(numden(near[c][0], heads[c][2], heads[c][:2], *grads[c], before, ()))
    scan = Scan(*nums[1][3:], True)

    def out_project(c, after):
        keep_a, keep_b, send_x, send_d = project(
            NN, *heads[c][:2], *gathered[c], weights, after
        )
        return (keep_a, keep_b), (to_d(send_d), to_x(send_x))

    parts = []

    def local_block(block, after):
        c = block // 2
        before = (parts[-1][0],) if parts else ()
        parts.append(
            local(
                near[c][0],
                fk,
                value_input,
                *nums[c][:2],
                loc,
                prior,
                block,
                before,
                after,
            )
        )
        return parts[-1][1]

    sent = scan.hop()
    done = local_block(0, (sent,))
    sent = scan.hop(done)
    done = local_block(1, (sent,))
    sent = scan.hop(done)
    out0 = out_project(0, (sent,))
    sent = scan.hop(out0[0][0])
    done = local_block(2, (sent, out0[0][0]))
    sent = scan.hop(done)
    out1 = out_project(1, (sent,))
    done = local_block(3, (out1[0][0],))
    scan.hop(done)
    out, grad_query, grad_key, grad_value = later(
        fk,
        value_input,
        parts[-1][0],
        *out0,
        [x for part in parts for x in part[1:]],
        nums[0][2],
        nums[1][2],
        scan.result(),
    )
    return finish(*out1, out), grad_query, grad_key, grad_value


def solution(mesh):
    in_specs = (
        P("ctx", "head"),
        P("ctx", "head"),
        P("ctx", "head"),
        P("head", None),
        P("ctx", "head"),
    )
    out_specs = (P("ctx", "head"), P("ctx", "head"), P("ctx", "head"), P("ctx", "head"))
    return jax.shard_map(
        on_device, mesh=mesh, in_specs=in_specs, out_specs=out_specs, check_vma=False
    )
```
